512 devices in a mesh: leaf: 8 (over y), row: 64 (over z, x, core).
Axes of the slice: x: 4, y: 8, z: 8, core: 2. Of those that a mesh axis runs over, the one named last changes fastest.
Arguments:
- rhs_field: float32 [64, 262144], P(None, ('leaf', 'row')), may hold values from -6 to 6
- right_basis: float32 [3, 256, 262144], P(None, None, ('leaf', 'row')), may hold values from -6 to 6
- left_basis: float32 [3, 256, 262144], P(None, None, ('leaf', 'row')), may hold values from -0.375 to 0.375
- cores: float32 [8, 3, 512, 256], P('leaf'), as said below
Outputs:
- solution: float32 [64, 262144], P(None, ('leaf', 'row'))
The draws below stay inside these ranges and needn't reach their ends.
Inputs may be any that keep to these rules, and one draw needn't show every extreme that they name: cores[i, k] is the same matrix for all i in one aligned block of 2**k indices; its entries have zero mean and magnitudes up to a few times 0.5 / sqrt(2 * 256 * 2**k * 32768).
All inputs are finite; a program needn't handle non-finite values.
Results may differ from the reference program's by a relative error of at most 0.0001.
Values sent between devices are 32-bit elements; how exact they have to be, the bound alone decides.
No kernel may reach another device: no remote copies, remote signals or barrier semaphores. Data moves between devices by JAX's collectives and lax.ppermute only.
A program may use at most 64 MiB of HBM per device.

```python
import math
import jax
import jax.numpy as jnp
from jax import lax

R = 256
NRHS = 64
ROWS_DEV = 512
DEPTH = 3
NPTS = 262144
N_LEAF = 8
N_ROW = 64


def draw_cores(key, part):
    key = jax.random.fold_in(key, 11)
    blocks = []
    for level in range(DEPTH):
        owners = jnp.arange(N_LEAF, dtype=jnp.int32) // 2 ** level
        level_key = jax.random.fold_in(key, level)
        keys = jax.vmap(lambda owner: jax.random.fold_in(level_key, owner))(owners)
        scale = 0.5 / math.sqrt(2.0 * R * 2 ** level * ROWS_DEV * N_ROW)
        values = jax.vmap(lambda k: jax.random.normal(k, (2 * R, R), jnp.float32))(keys)
        blocks.append(values * scale)
    return jnp.stack(blocks, axis=1)


def shard_levels(key, shape, shards, low, largest):
    loudness = 1.0
    for position, blocks in shards:
        steps = jax.random.uniform(jax.random.fold_in(jax.random.fold_in(key, 6), position), (blocks,), jnp.float32, low / len(shards), largest / len(shards))
        loudness = loudness * jnp.repeat(jnp.exp(steps), shape[position] // blocks).reshape((-1,) + (1,) * (len(shape) - 1 - position))
    return loudness


def bell_draw(stream_key, extent, deviation, reach, shards=(), kind=jnp.bfloat16):
    entries = jax.random.normal(stream_key, extent, jnp.float32) * deviation
    if len(shards) > 0:
        entries = shard_levels(stream_key, extent, shards, -0.22, 0.18) * entries
    return jnp.clip(entries, min=-reach, max=reach).astype(kind)


def setup_inputs(seed: int = 0) -> dict:
    streams_of = jax.random.split(jax.random.key(seed), 5)
    return {
        "rhs_field": bell_draw(streams_of[0], (NRHS, NPTS), 1.0, 6.0, ((1, 512),), jnp.float32),
        "right_basis": bell_draw(streams_of[1], (DEPTH, R, NPTS), 1.0, 6.0, ((2, 512),), jnp.float32),
        "left_basis": bell_draw(streams_of[2], (DEPTH, R, NPTS), R ** -0.5, 0.375, ((2, 512),), jnp.float32),
        "cores": draw_cores(jax.random.fold_in(streams_of[4], 71), 0),
    }


def reference(rhs_field, right_basis, left_basis, cores):
    precise = lax.Precision.HIGHEST
    field = rhs_field
    for level in range(DEPTH):
        span = (2 ** level) * ROWS_DEV * N_ROW
        blocks = NPTS // span
        shaped = field.reshape(NRHS, blocks, span)
        basis = right_basis[level].reshape(R, blocks, span)
        proj = jnp.einsum('nbs,rbs->bnr', shaped, basis, precision=precise)
        pairs = proj.reshape(blocks // 2, 2, NRHS, R)
        stacked = jnp.concatenate([pairs[:, 0], pairs[:, 1]], axis=2)
        stacked = jnp.repeat(stacked, 2, axis=0)
        rows_core = cores[::2 ** level, level]
        coeff = jnp.einsum('bnq,bqr->bnr', stacked, rows_core, precision=precise)
        update = jnp.einsum('bnr,rbs->nbs', coeff, left_basis[level].reshape(R, blocks, span), precision=precise)
        field = field - update.reshape(NRHS, NPTS)
    return field
```

```python
import jax
import jax.numpy as jnp
from jax import lax
from jax.experimental import pallas as pl
from jax.experimental.pallas import tpu as pltpu
from jax.sharding import Mesh, PartitionSpec as P

LEAF = ("y2", "y1", "y0")
HALF = 16
LANES = 128


def mul(a, b):
    return lax.dot_general(
        a,
        b,
        (((1,), (0,)), ((), ())),
        precision=lax.Precision.HIGHEST,
        preferred_element_type=jnp.float32,
    )


def mul_t(a, b):
    return lax.dot_general(
        a,
        b,
        (((1,), (1,)), ((), ())),
        precision=lax.Precision.HIGHEST,
        preferred_element_type=jnp.float32,
    )


def gram_kernel(field_ref, right_ref, left_ref, out_ref):
    field = field_ref[...]
    peers = out_ref.shape[0]

    def put_packed(block, row, value):
        for s in range(peers):
            top = value[HALF * s : HALF * (s + 1)]
            low = value[LANES + HALF * s : LANES + HALF * (s + 1)]
            out_ref[s, block, row : row + HALF, :] = jnp.concatenate([top, low], axis=1)

    def put(block, value):
        for s in range(peers):
            for h in range(2):
                out_ref[s, block, HALF * h : HALF * (h + 1), :] = value[
                    LANES * h + HALF * s : LANES * h + HALF * (s + 1)
                ]

    put_packed(0, 0, mul_t(right_ref[0], field))
    put_packed(0, HALF, mul_t(right_ref[1], field))
    put_packed(1, 0, mul_t(right_ref[2], field))
    for s in range(peers):
        out_ref[s, 1, HALF:, :] = jnp.zeros((HALF, LANES), jnp.float32)
    block = 2
    for j, k in ((0, 1), (0, 2), (1, 2)):
        gram = mul_t(right_ref[k], left_ref[j])
        put(block, gram[:, :LANES])
        put(block + 1, gram[:, LANES:])
        block += 2


def sum_kernel(in_ref, out_ref):
    total = in_ref[0]
    for s in range(1, in_ref.shape[0]):
        total = total + in_ref[s]
    out_ref[...] = total


def sum_spread_kernel(in_ref, out_ref):
    total = in_ref[0]
    for s in range(1, in_ref.shape[0]):
        total = total + in_ref[s]
    for s in range(out_ref.shape[0]):
        out_ref[s] = total


def coefficients(got_ref, core_ref):
    sides = []
    group = got_ref.shape[0] // 2
    for side in range(2):
        part = got_ref[side * group]
        for g in range(1, group):
            part = part + got_ref[side * group + g]
        turned = part.reshape(LANES, LANES).T
        sides += [turned[: LANES // 2], turned[LANES // 2 :]]
    stacked = jnp.concatenate(sides, axis=1)
    return mul(stacked, core_ref[0, 0])


def packed(value):
    return jnp.concatenate([value[:HALF], value[HALF:]], axis=1)


def gram_block(blocks_ref, first):
    return jnp.concatenate([blocks_ref[first], blocks_ref[first + 1]], axis=1)


def level0_kernel(got_ref, core_ref, blocks_ref, coeff_ref, out_ref):
    coeff = coefficients(got_ref, core_ref)
    coeff_ref[...] = coeff
    fresh = blocks_ref[0, HALF:, :] - packed(mul_t(gram_block(blocks_ref, 2), coeff))
    for s in range(out_ref.shape[0]):
        out_ref[s] = fresh


def level1_kernel(got_ref, core_ref, blocks_ref, coeff0_ref, coeff_ref, out_ref):
    coeff = coefficients(got_ref, core_ref)
    coeff_ref[...] = coeff
    change = mul_t(gram_block(blocks_ref, 4), coeff0_ref[...])
    change = change + mul_t(gram_block(blocks_ref, 6), coeff)
    fresh = blocks_ref[1, :HALF, :] - packed(change)
    for s in range(out_ref.shape[0]):
        out_ref[s] = fresh


def level2_kernel(got_ref, core_ref, coeff0_ref, coeff1_ref, field_ref, left_ref, out_ref):
    change = mul(coeff0_ref[...], left_ref[0]) + mul(coeff1_ref[...], left_ref[1])
    coeff = coefficients(got_ref, core_ref)
    change = change + mul(coeff, left_ref[2])
    out_ref[...] = field_ref[...] - change


def whole(x):
    return pl.BlockSpec(x.shape, lambda i: (0,) * x.ndim)


def core_of(cores, level):
    return pl.BlockSpec((1, 1) + cores.shape[2:], lambda i: (0, level, 0, 0))


def call(kernel, out_shape, args, in_specs=None):
    if in_specs is None:
        in_specs = [whole(x) for x in args]
    single = not isinstance(out_shape[0], tuple)
    shapes = (out_shape,) if single else out_shape
    out = tuple(jax.ShapeDtypeStruct(s, jnp.float32) for s in shapes)
    specs = tuple(whole(o) for o in out)
    return pl.pallas_call(
        kernel,
        grid=(1,),
        out_shape=out[0] if single else out,
        in_specs=in_specs,
        out_specs=specs[0] if single else specs,
        compiler_params=pltpu.CompilerParams(vmem_limit_bytes=32 << 20),
    )(*args)


def swap(x, axes):
    return lax.all_to_all(x, axes, 0, 0, tiled=True)


def shards(rhs_field, right_basis, left_basis, cores):
    nz, ns = lax.axis_size("z"), lax.axis_size("xc")
    tile = (2 * HALF, LANES)
    half = (HALF, LANES)
    rhs, rank = rhs_field.shape[0], right_basis.shape[1]

    part = call(gram_kernel, (ns, nz) + tile, (rhs_field, right_basis, left_basis))
    part = swap(part, "xc")
    part = call(sum_kernel, (nz,) + tile, (part,))
    part = swap(part, "z")
    part = call(sum_spread_kernel, (nz,) + tile, (part,))
    blocks = swap(part, "z")

    send = jnp.broadcast_to(blocks[0, :HALF], (2 * ns,) + half)
    got = swap(send, ("y0", "xc")).reshape((2, ns) + half)
    coeff0, send = call(
        level0_kernel,
        ((rhs, rank), (4 * ns,) + half),
        (got, cores, blocks),
        [whole(got), core_of(cores, 0), whole(blocks)],
    )
    got = swap(send, ("y1", "y0", "xc")).reshape((4, ns) + half)
    coeff1, send = call(
        level1_kernel,
        ((rhs, rank), (8 * ns,) + half),
        (got, cores, blocks, coeff0),
        [whole(got), core_of(cores, 1), whole(blocks), whole(coeff0)],
    )
    got = swap(send, ("y2", "y1", "y0", "xc")).reshape((8, ns) + half)
    return call(
        level2_kernel,
        rhs_field.shape,
        (got, cores, coeff0, coeff1, rhs_field, left_basis),
        [whole(got), core_of(cores, 2), whole(coeff0), whole(coeff1), whole(rhs_field), whole(left_basis)],
    )


def solution(mesh):
    ns = 8
    devices = mesh.devices.reshape((2, 2, 2, mesh.shape["row"] // ns, ns))
    fine = Mesh(devices, LEAF + ("z", "xc"))
    points = LEAF + ("z", "xc")
    in_specs = (
        P(None, points),
        P(None, None, points),
        P(None, None, points),
        P(LEAF, None, None, None),
    )
    return jax.shard_map(shards, mesh=fine, in_specs=in_specs, out_specs=P(None, points), check_vma=False)
```

```python
import functools

import jax
import jax.numpy as jnp
from jax import lax
from jax.experimental import pallas as pl
from jax.experimental.pallas import tpu as pltpu
from jax.sharding import Mesh, PartitionSpec as P

LEAF = ("y2", "y1", "y0")
CHIP = ("c", "x")
HALF = 16
LANES = 128
BLOCKS = 8


def halves(a):
    high = a.astype(jnp.bfloat16)
    return high, (a - high.astype(jnp.float32)).astype(jnp.bfloat16)


def product(a, b, dims):
    def one(u, v):
        return lax.dot_general(u, v, (dims, ((), ())), preferred_element_type=jnp.float32)

    return one(a[0], b[0]) + (one(a[0], b[1]) + one(a[1], b[0]))


def mul(a, b):
    return product(halves(a), halves(b), ((1,), (0,)))


def mul_t(a, b):
    return product(halves(a), halves(b), ((1,), (1,)))


def gram_kernel(own, field_hbm, right_hbm, left_hbm, out_ref, field, right, left, sems):
    core = lax.axis_index("c")
    side = core if own else 1 - core
    depth, _, rows = right.shape[:3]
    copies = []

    def fetch(src, dst):
        copy = pltpu.make_async_copy(src, dst, sems.at[len(copies)])
        copy.start()
        copies.append(copy)
        return copy

    got_field = fetch(field_hbm, field)
    got_right = [
        [fetch(right_hbm.at[k, pl.ds(2 * rows * h + rows * side, rows), :], right.at[k, h]) for h in range(2)]
        for k in range(depth)
    ]
    got_left = [fetch(left_hbm.at[j], left.at[j]) for j in range(left.shape[0])]
    peers = out_ref.shape[0]

    def put_packed(block, row, value):
        for s in range(peers):
            top = value[HALF * s : HALF * (s + 1)]
            low = value[rows + HALF * s : rows + HALF * (s + 1)]
            out_ref[s, block, row : row + HALF, :] = jnp.concatenate([top, low], axis=1)

    def put(block, value):
        for s in range(peers):
            for h in range(2):
                out_ref[s, block, HALF * h : HALF * (h + 1), :] = value[
                    rows * h + HALF * s : rows * h + HALF * (s + 1)
                ]

    for s in range(peers):
        out_ref[s, 1, HALF:, :] = jnp.zeros((HALF, LANES), jnp.float32)
    got_field.wait()
    rhs = halves(field[...])
    mine = []
    for k in range(depth):
        for h in range(2):
            got_right[k][h].wait()
        mine.append(halves(right[k].reshape(2 * rows, right.shape[3])))
        put_packed(k // 2, HALF * (k % 2), product(mine[k], rhs, ((1,), (1,))))
    for j in range(left.shape[0]):
        got_left[j].wait()
        other = halves(left[j])
        for k in range(j + 1, depth):
            gram = product(mine[k], other, ((1,), (1,)))
            block = 2 * (j + k)
            put(block, gram[:, :LANES])
            put(block + 1, gram[:, LANES:])


def gram_rows(own, field, right, left):
    depth, rank, points = right.shape
    rows = rank // 4
    scratch = [
        pltpu.VMEM(field.shape, jnp.float32),
        pltpu.VMEM((depth, 2, rows, points), jnp.float32),
        pltpu.VMEM((depth - 1, rank, points), jnp.float32),
        pltpu.SemaphoreType.DMA((1 + 2 * depth + depth - 1,)),
    ]
    return pl.pallas_call(
        functools.partial(gram_kernel, own),
        out_shape=jax.ShapeDtypeStruct((rows // HALF, BLOCKS, 2 * HALF, LANES), jnp.float32),
        in_specs=[pl.BlockSpec(memory_space=pltpu.HBM)] * 3,
        out_specs=pl.BlockSpec(memory_space=pltpu.VMEM),
        scratch_shapes=scratch,
        cost_estimate=pl.CostEstimate(flops=800_000_000, bytes_accessed=2_500_000, transcendentals=0),
        compiler_params=pltpu.CompilerParams(vmem_limit_bytes=54000 << 10),
    )(field, right, left)


def add_kernel(a_ref, b_ref, out_ref):
    out_ref[...] = a_ref[...] + b_ref[...]


def sum_kernel(in_ref, out_ref):
    total = in_ref[0]
    for s in range(1, in_ref.shape[0]):
        total = total + in_ref[s]
    out_ref[...] = total


def sum_spread_kernel(in_ref, out_ref):
    total = in_ref[0]
    for s in range(1, in_ref.shape[0]):
        total = total + in_ref[s]
    for s in range(out_ref.shape[0]):
        out_ref[s] = total


def coefficients(parts, core_ref):
    sides = []
    for part in parts:
        turned = part.reshape(LANES, LANES).T
        sides += [turned[: LANES // 2], turned[LANES // 2 :]]
    return mul(jnp.concatenate(sides, axis=1), core_ref[0, 0])


def two_sides(got_ref):
    group = got_ref.shape[0] // 2
    parts = []
    for side in range(2):
        part = got_ref[side * group]
        for g in range(1, group):
            part = part + got_ref[side * group + g]
        parts.append(part)
    return parts


def quads_kernel(got_ref, out_ref):
    for side, part in enumerate(two_sides(got_ref)):
        for s in range(out_ref.shape[0]):
            out_ref[s, side] = part


def packed(value):
    return jnp.concatenate([value[:HALF], value[HALF:]], axis=1)


def gram_block(blocks_ref, first):
    return jnp.concatenate([blocks_ref[first], blocks_ref[first + 1]], axis=1)


def level0_kernel(got_ref, core_ref, blocks_ref, coeff_ref, out_ref):
    coeff = coefficients(two_sides(got_ref), core_ref)
    coeff_ref[...] = coeff
    fresh = blocks_ref[0, HALF:, :] - packed(mul_t(gram_block(blocks_ref, 2), coeff))
    for s in range(out_ref.shape[0]):
        out_ref[s] = fresh


def level1_kernel(got_ref, core_ref, blocks_ref, coeff0_ref, coeff_ref, out_ref):
    coeff = coefficients(two_sides(got_ref), core_ref)
    coeff_ref[...] = coeff
    change = mul_t(gram_block(blocks_ref, 4), coeff0_ref[...])
    change = change + mul_t(gram_block(blocks_ref, 6), coeff)
    fresh = blocks_ref[1, :HALF, :] - packed(change)
    for s in range(out_ref.shape[0]):
        out_ref[s] = fresh


def level2_kernel(got_ref, core_ref, coeff0_ref, coeff1_ref, field_ref, left_ref, out_ref):
    change = mul(coeff0_ref[...], left_ref[0]) + mul(coeff1_ref[...], left_ref[1])
    coeff = coefficients([got_ref[:, 0], got_ref[:, 1]], core_ref)
    change = change + mul(coeff, left_ref[2])
    out_ref[...] = field_ref[...] - change


def whole(x):
    return pl.BlockSpec(x.shape, lambda i: (0,) * x.ndim)


def core_of(cores, level):
    return pl.BlockSpec((1, 1) + cores.shape[2:], lambda i: (0, level, 0, 0))


def call(kernel, out_shape, args, in_specs=None):
    if in_specs is None:
        in_specs = [whole(x) for x in args]
    single = not isinstance(out_shape[0], tuple)
    shapes = (out_shape,) if single else out_shape
    out = tuple(jax.ShapeDtypeStruct(s, jnp.float32) for s in shapes)
    specs = tuple(whole(o) for o in out)
    return pl.pallas_call(
        kernel,
        grid=(1,),
        out_shape=out[0] if single else out,
        in_specs=in_specs,
        out_specs=specs[0] if single else specs,
        compiler_params=pltpu.CompilerParams(vmem_limit_bytes=32 << 20),
    )(*args)


def swap(x, axes):
    return lax.all_to_all(x, axes, 0, 0, tiled=True)


def shards(rhs_field, right_basis, left_basis, cores):
    nz, nx = lax.axis_size("z"), lax.axis_size("x")
    ns = 2 * nx
    tile = (2 * HALF, LANES)
    half = (HALF, LANES)
    rhs, rank = rhs_field.shape[0], right_basis.shape[1]

    theirs = gram_rows(False, rhs_field, right_basis, left_basis)
    theirs = lax.ppermute(theirs, "c", [(0, 1), (1, 0)])
    mine = gram_rows(True, rhs_field, right_basis, left_basis)
    part = call(add_kernel, mine.shape, (mine, theirs))
    part = swap(part, "x")
    part = call(sum_kernel, (nz,) + tile, (part,))
    part = swap(part, "z")
    part = call(sum_spread_kernel, (nz,) + tile, (part,))
    blocks = swap(part, "z")

    send = jnp.broadcast_to(blocks[0, :HALF], (2 * ns,) + half)
    got = swap(send, ("y0",) + CHIP).reshape((2, ns) + half)
    coeff0, send = call(
        level0_kernel,
        ((rhs, rank), (4 * ns,) + half),
        (got, cores, blocks),
        [whole(got), core_of(cores, 0), whole(blocks)],
    )
    got = swap(send, ("y1", "y0") + CHIP).reshape((4, ns) + half)
    coeff1, send = call(
        level1_kernel,
        ((rhs, rank), (8,) + half),
        (got, cores, blocks, coeff0),
        [whole(got), core_of(cores, 1), whole(blocks), whole(coeff0)],
    )
    got = swap(send, LEAF)
    send = call(quads_kernel, (ns, 2) + half, (got,))
    got = swap(send, CHIP)
    return call(
        level2_kernel,
        rhs_field.shape,
        (got, cores, coeff0, coeff1, rhs_field, left_basis),
        [whole(got), core_of(cores, 2), whole(coeff0), whole(coeff1), whole(rhs_field), whole(left_basis)],
    )


def solution(mesh):
    nx, cores_of_chip = 4, 2
    nz = mesh.shape["row"] // (nx * cores_of_chip)
    points = LEAF + ("z", "x", "c")
    fine = Mesh(mesh.devices.reshape((2, 2, 2, nz, nx, cores_of_chip)), points)
    in_specs = (
        P(None, points),
        P(None, None, points),
        P(None, None, points),
        P(LEAF, None, None, None),
    )
    return jax.shard_map(shards, mesh=fine, in_specs=in_specs, out_specs=P(None, points), check_vma=False)
```

```python
import jax
import jax.numpy as jnp
from jax import lax
from jax.experimental import pallas as pl
from jax.experimental.pallas import tpu as pltpu
from jax.sharding import Mesh, PartitionSpec as P

LEAF = ("y2", "y1", "y0")
CHIP = ("c", "x")
HALF = 16
LANES = 128
BLOCKS = 8


def halves(a):
    high = a.astype(jnp.bfloat16)
    return high, (a - high.astype(jnp.float32)).astype(jnp.bfloat16)


def product(a, b, dims):
    def one(u, v):
        return lax.dot_general(u, v, (dims, ((), ())), preferred_element_type=jnp.float32)

    return one(a[0], b[0]) + (one(a[0], b[1]) + one(a[1], b[0]))


def mul(a, b):
    return product(halves(a), halves(b), ((1,), (0,)))


def mul_t(a, b):
    return product(halves(a), halves(b), ((1,), (1,)))


def stacked_product(a_high, a_low, b):
    rows = a_high.shape[0]

    def one(u, v):
        return lax.dot_general(u, v, (((1,), (1,)), ((), ())), preferred_element_type=jnp.float32)

    both = one(jnp.concatenate([a_high, a_low], axis=0), b[0])
    return both[:rows] + (both[rows:] + one(a_high, b[1]))


def gram_kernel(field_hbm, right_hbm, left_hbm, theirs_ref, mine_ref, field, right, left, sems):
    core = lax.axis_index("c")
    sides = (1 - core, core)
    outs = (theirs_ref, mine_ref)
    depth, _, _, rows, points = right.shape
    peers = mine_ref.shape[0]
    copies = []

    def fetch(src, dst):
        copy = pltpu.make_async_copy(src, dst, sems.at[len(copies)])
        copy.start()
        copies.append(copy)
        return copy

    def fetch_right(k):
        return [
            fetch(right_hbm.at[k, pl.ds(2 * rows * h + rows * side, rows), :], right.at[k, slot, h])
            for slot, side in enumerate(sides)
            for h in range(2)
        ]

    def fetch_left(j):
        part = left.shape[1] // 2
        return [fetch(left_hbm.at[j, pl.ds(part * i, part), :], left.at[j, pl.ds(part * i, part), :]) for i in range(2)]

    got_left, got_right = {}, {}
    got_left[0] = fetch_left(0)
    got_right[1] = fetch_right(1)
    got_right[2] = fetch_right(2)
    got_left[1] = fetch_left(1)
    got_field = fetch(field_hbm, field)
    got_right[0] = fetch_right(0)

    def arrived(waits):
        for copy in waits:
            copy.wait()

    def basis(k):
        arrived(got_right[k])
        return halves(right[k].reshape(4 * rows, points))

    def put(k, block, value):
        for slot, out_ref in enumerate(outs):
            for s in range(peers):
                for h in range(2):
                    first = 4 * rows * k + 2 * rows * slot + rows * h + HALF * s
                    piece = value[first : first + HALF]
                    out_ref[s, block, HALF * h : HALF * (h + 1), :] = piece[:, :LANES]
                    out_ref[s, block + 1, HALF * h : HALF * (h + 1), :] = piece[:, LANES:]

    def put_packed(k, value):
        for slot, out_ref in enumerate(outs):
            for s in range(peers):
                first = 4 * rows * k + 2 * rows * slot + HALF * s
                piece = [value[first + rows * h : first + rows * h + HALF] for h in range(2)]
                out_ref[s, k // 2, HALF * (k % 2) : HALF * (k % 2 + 1), :] = jnp.concatenate(piece, axis=1)

    for out_ref in outs:
        for s in range(peers):
            out_ref[s, 1, HALF:, :] = jnp.zeros((HALF, LANES), jnp.float32)
    arrived(got_left[0])
    first_left = halves(left[0])
    one, two = basis(1), basis(2)
    high, low = (jnp.concatenate([one[i], two[i]], axis=0) for i in range(2))
    gram = stacked_product(high, low, first_left)
    put(0, 2, gram)
    put(1, 4, gram)
    arrived(got_left[1])
    put(0, 6, stacked_product(two[0], two[1], halves(left[1])))
    got_field.wait()
    zero = basis(0)
    high, low = (jnp.concatenate([zero[i], one[i], two[i]], axis=0) for i in range(2))
    proj = stacked_product(high, low, halves(field[...]))
    for k in range(depth):
        put_packed(k, proj)


def gram_rows(field, right, left):
    depth, rank, points = right.shape
    rows = rank // 4
    out = jax.ShapeDtypeStruct((rows // HALF, BLOCKS, 2 * HALF, LANES), jnp.float32)
    return pl.pallas_call(
        gram_kernel,
        out_shape=(out, out),
        in_specs=[pl.BlockSpec(memory_space=pltpu.HBM)] * 3,
        out_specs=(pl.BlockSpec(memory_space=pltpu.VMEM),) * 2,
        scratch_shapes=[
            pltpu.VMEM(field.shape, jnp.float32),
            pltpu.VMEM((depth, 2, 2, rows, points), jnp.float32),
            pltpu.VMEM((depth - 1, rank, points), jnp.float32),
            pltpu.SemaphoreType.DMA((1 + 4 * depth + 2 * (depth - 1),)),
        ],
        compiler_params=pltpu.CompilerParams(vmem_limit_bytes=54000 << 10),
    )(field, right, left)


def add_kernel(a_ref, b_ref, out_ref):
    out_ref[...] = a_ref[...] + b_ref[...]


def sum_kernel(in_ref, out_ref):
    total = in_ref[0]
    for s in range(1, in_ref.shape[0]):
        total = total + in_ref[s]
    out_ref[...] = total


def sum_spread_kernel(in_ref, out_ref):
    total = in_ref[0]
    for s in range(1, in_ref.shape[0]):
        total = total + in_ref[s]
    for s in range(out_ref.shape[0]):
        out_ref[s] = total


def coefficients(parts, core_ref):
    sides = []
    for part in parts:
        turned = part.reshape(LANES, LANES).T
        sides += [turned[: LANES // 2], turned[LANES // 2 :]]
    return mul(jnp.concatenate(sides, axis=1), core_ref[0, 0])


def two_sides(got_ref):
    group = got_ref.shape[0] // 2
    parts = []
    for side in range(2):
        part = got_ref[side * group]
        for g in range(1, group):
            part = part + got_ref[side * group + g]
        parts.append(part)
    return parts


def quads_kernel(got_ref, out_ref):
    for side, part in enumerate(two_sides(got_ref)):
        for s in range(out_ref.shape[0]):
            out_ref[s, side] = part


def packed(value):
    return jnp.concatenate([value[:HALF], value[HALF:]], axis=1)


def gram_block(blocks_ref, first):
    return jnp.concatenate([blocks_ref[first], blocks_ref[first + 1]], axis=1)


def level0_kernel(got_ref, core_ref, blocks_ref, coeff_ref, out_ref):
    coeff = coefficients(two_sides(got_ref), core_ref)
    coeff_ref[...] = coeff
    fresh = blocks_ref[0, HALF:, :] - packed(mul_t(gram_block(blocks_ref, 2), coeff))
    for s in range(out_ref.shape[0]):
        out_ref[s] = fresh


def level1_kernel(got_ref, core_ref, blocks_ref, coeff0_ref, coeff_ref, out_ref):
    coeff = coefficients(two_sides(got_ref), core_ref)
    coeff_ref[...] = coeff
    change = mul_t(gram_block(blocks_ref, 4), coeff0_ref[...])
    change = change + mul_t(gram_block(blocks_ref, 6), coeff)
    fresh = blocks_ref[1, :HALF, :] - packed(change)
    for s in range(out_ref.shape[0]):
        out_ref[s] = fresh


def level2_kernel(got_ref, core_ref, coeff0_ref, coeff1_ref, field_ref, left_ref, out_ref):
    change = mul(coeff0_ref[...], left_ref[0]) + mul(coeff1_ref[...], left_ref[1])
    coeff = coefficients([got_ref[:, 0], got_ref[:, 1]], core_ref)
    change = change + mul(coeff, left_ref[2])
    out_ref[...] = field_ref[...] - change


def whole(x):
    return pl.BlockSpec(x.shape, lambda i: (0,) * x.ndim)


def core_of(cores, level):
    return pl.BlockSpec((1, 1) + cores.shape[2:], lambda i: (0, level, 0, 0))


def call(kernel, out_shape, args, in_specs=None):
    if in_specs is None:
        in_specs = [whole(x) for x in args]
    single = not isinstance(out_shape[0], tuple)
    shapes = (out_shape,) if single else out_shape
    out = tuple(jax.ShapeDtypeStruct(s, jnp.float32) for s in shapes)
    specs = tuple(whole(o) for o in out)
    return pl.pallas_call(
        kernel,
        grid=(1,),
        out_shape=out[0] if single else out,
        in_specs=in_specs,
        out_specs=specs[0] if single else specs,
        compiler_params=pltpu.CompilerParams(vmem_limit_bytes=32 << 20),
    )(*args)


def swap(x, axes):
    return lax.all_to_all(x, axes, 0, 0, tiled=True)


def shards(rhs_field, right_basis, left_basis, cores):
    nz, nx = lax.axis_size("z"), lax.axis_size("x")
    ns = 2 * nx
    tile = (2 * HALF, LANES)
    half = (HALF, LANES)
    rhs, rank = rhs_field.shape[0], right_basis.shape[1]

    theirs, mine = gram_rows(rhs_field, right_basis, left_basis)
    theirs = lax.ppermute(theirs, "c", [(0, 1), (1, 0)])
    part = call(add_kernel, mine.shape, (mine, theirs))
    part = swap(part, "x")
    part = call(sum_kernel, (nz,) + tile, (part,))
    part = swap(part, "z")
    part = call(sum_spread_kernel, (nz,) + tile, (part,))
    blocks = swap(part, "z")

    send = jnp.broadcast_to(blocks[0, :HALF], (2 * ns,) + half)
    got = swap(send, ("y0",) + CHIP).reshape((2, ns) + half)
    coeff0, send = call(
        level0_kernel,
        ((rhs, rank), (4 * ns,) + half),
        (got, cores, blocks),
        [whole(got), core_of(cores, 0), whole(blocks)],
    )
    got = swap(send, ("y1", "y0") + CHIP).reshape((4, ns) + half)
    coeff1, send = call(
        level1_kernel,
        ((rhs, rank), (8,) + half),
        (got, cores, blocks, coeff0),
        [whole(got), core_of(cores, 1), whole(blocks), whole(coeff0)],
    )
    got = swap(send, LEAF)
    send = call(quads_kernel, (ns, 2) + half, (got,))
    got = swap(send, CHIP)
    return call(
        level2_kernel,
        rhs_field.shape,
        (got, cores, coeff0, coeff1, rhs_field, left_basis),
        [whole(got), core_of(cores, 2), whole(coeff0), whole(coeff1), whole(rhs_field), whole(left_basis)],
    )


def solution(mesh):
    nx, cores_of_chip = 4, 2
    nz = mesh.shape["row"] // (nx * cores_of_chip)
    points = LEAF + ("z", "x", "c")
    fine = Mesh(mesh.devices.reshape((2, 2, 2, nz, nx, cores_of_chip)), points)
    in_specs = (
        P(None, points),
        P(None, None, points),
        P(None, None, points),
        P(LEAF, None, None, None),
    )
    return jax.shard_map(shards, mesh=fine, in_specs=in_specs, out_specs=P(None, points), check_vma=False)
```

```python
import jax
import jax.numpy as jnp
from jax import lax
from jax.experimental import pallas as pl
from jax.experimental.pallas import tpu as pltpu
from jax.sharding import Mesh, PartitionSpec as P

LEAF = ("y2", "y1", "y0")
CHIP = ("c", "x")
HALF = 16
LANES = 128
BLOCKS = 8


def halves(a):
    high = a.astype(jnp.bfloat16)
    return high, (a - high.astype(jnp.float32)).astype(jnp.bfloat16)


def product(a, b, dims):
    def one(u, v):
        return lax.dot_general(u, v, (dims, ((), ())), preferred_element_type=jnp.float32)

    return one(a[0], b[0]) + (one(a[0], b[1]) + one(a[1], b[0]))


def mul(a, b):
    return product(halves(a), halves(b), ((1,), (0,)))


def mul_t(a, b):
    return product(halves(a), halves(b), ((1,), (1,)))


def stacked_product(a_high, a_low, b):
    rows = a_high.shape[0]

    def one(u, v):
        return lax.dot_general(u, v, (((1,), (1,)), ((), ())), preferred_element_type=jnp.float32)

    both = one(jnp.concatenate([a_high, a_low], axis=0), b[0])
    return both[:rows] + (both[rows:] + one(a_high, b[1]))


def gram_kernel(field_hbm, right_hbm, left_hbm, theirs_ref, mine_ref, field, right, left, sems):
    core = lax.axis_index("c")
    sides = (1 - core, core)
    outs = (theirs_ref, mine_ref)
    depth, _, _, rows, points = right.shape
    peers = mine_ref.shape[0]
    copies = []

    def fetch(src, dst):
        copy = pltpu.make_async_copy(src, dst, sems.at[len(copies)])
        copy.start()
        copies.append(copy)
        return copy

    def fetch_right(k):
        return [
            fetch(right_hbm.at[k, pl.ds(2 * rows * h + rows * side, rows), :], right.at[k, slot, h])
            for slot, side in enumerate(sides)
            for h in range(2)
        ]

    def fetch_left(j):
        part = left.shape[1] // 2
        return [fetch(left_hbm.at[j, pl.ds(part * i, part), :], left.at[j, pl.ds(part * i, part), :]) for i in range(2)]

    got_left, got_right = {}, {}
    got_left[0] = fetch_left(0)
    got_right[1] = fetch_right(1)
    got_right[2] = fetch_right(2)
    got_left[1] = fetch_left(1)
    got_field = fetch(field_hbm, field)
    got_right[0] = fetch_right(0)

    def arrived(waits):
        for copy in waits:
            copy.wait()

    def basis(k):
        arrived(got_right[k])
        return halves(right[k].reshape(4 * rows, points))

    def put(k, block, value):
        for slot, out_ref in enumerate(outs):
            for s in range(peers):
                for h in range(2):
                    first = 4 * rows * k + 2 * rows * slot + rows * h + HALF * s
                    piece = value[first : first + HALF]
                    out_ref[s, block, HALF * h : HALF * (h + 1), :] = piece[:, :LANES]
                    out_ref[s, block + 1, HALF * h : HALF * (h + 1), :] = piece[:, LANES:]

    def put_packed(k, value):
        for slot, out_ref in enumerate(outs):
            for s in range(peers):
                first = 4 * rows * k + 2 * rows * slot + HALF * s
                piece = [value[first + rows * h : first + rows * h + HALF] for h in range(2)]
                out_ref[s, k // 2, HALF * (k % 2) : HALF * (k % 2 + 1), :] = jnp.concatenate(piece, axis=1)

    for out_ref in outs:
        for s in range(peers):
            out_ref[s, 1, HALF:, :] = jnp.zeros((HALF, LANES), jnp.float32)
    arrived(got_left[0])
    first_left = halves(left[0])
    one, two = basis(1), basis(2)
    high, low = (jnp.concatenate([one[i], two[i]], axis=0) for i in range(2))
    gram = stacked_product(high, low, first_left)
    put(0, 2, gram)
    put(1, 4, gram)
    arrived(got_left[1])
    put(0, 6, stacked_product(two[0], two[1], halves(left[1])))
    got_field.wait()
    zero = basis(0)
    high, low = (jnp.concatenate([zero[i], one[i], two[i]], axis=0) for i in range(2))
    proj = stacked_product(high, low, halves(field[...]))
    for k in range(depth):
        put_packed(k, proj)


def gram_rows(field, right, left):
    depth, rank, points = right.shape
    rows = rank // 4
    out = jax.ShapeDtypeStruct((rows // HALF, BLOCKS, 2 * HALF, LANES), jnp.float32)
    return pl.pallas_call(
        gram_kernel,
        out_shape=(out, out),
        in_specs=[pl.BlockSpec(memory_space=pltpu.HBM)] * 3,
        out_specs=(pl.BlockSpec(memory_space=pltpu.VMEM),) * 2,
        scratch_shapes=[
            pltpu.VMEM(field.shape, jnp.float32),
            pltpu.VMEM((depth, 2, 2, rows, points), jnp.float32),
            pltpu.VMEM((depth - 1, rank, points), jnp.float32),
            pltpu.SemaphoreType.DMA((1 + 4 * depth + 2 * (depth - 1),)),
        ],
        compiler_params=pltpu.CompilerParams(vmem_limit_bytes=54000 << 10),
    )(field, right, left)


def add_kernel(a_ref, b_ref, out_ref):
    out_ref[...] = a_ref[...] + b_ref[...]


def sum_spread_kernel(in_ref, out_ref):
    total = in_ref[0]
    for s in range(1, in_ref.shape[0]):
        total = total + in_ref[s]
    for s in range(out_ref.shape[0]):
        out_ref[s] = total


def coefficients(parts, core_ref):
    sides = []
    for part in parts:
        turned = part.reshape(LANES, LANES).T
        sides += [turned[: LANES // 2], turned[LANES // 2 :]]
    return mul(jnp.concatenate(sides, axis=1), core_ref[0, 0])


def two_sides(got_ref):
    group = got_ref.shape[0] // 2
    parts = []
    for side in range(2):
        part = got_ref[side * group]
        for g in range(1, group):
            part = part + got_ref[side * group + g]
        parts.append(part)
    return parts


def quads_kernel(got_ref, out_ref):
    for side, part in enumerate(two_sides(got_ref)):
        for s in range(out_ref.shape[0]):
            out_ref[s, side] = part


def packed(value):
    return jnp.concatenate([value[:HALF], value[HALF:]], axis=1)


def gram_block(blocks_ref, first):
    return jnp.concatenate([blocks_ref[first], blocks_ref[first + 1]], axis=1)


def level0_kernel(got_ref, core_ref, blocks_ref, coeff_ref, out_ref):
    coeff = coefficients(two_sides(got_ref), core_ref)
    coeff_ref[...] = coeff
    fresh = blocks_ref[0, HALF:, :] - packed(mul_t(gram_block(blocks_ref, 2), coeff))
    for s in range(out_ref.shape[0]):
        out_ref[s] = fresh


def level1_kernel(got_ref, core_ref, blocks_ref, coeff0_ref, coeff_ref, out_ref):
    coeff = coefficients(two_sides(got_ref), core_ref)
    coeff_ref[...] = coeff
    change = mul_t(gram_block(blocks_ref, 4), coeff0_ref[...])
    change = change + mul_t(gram_block(blocks_ref, 6), coeff)
    fresh = blocks_ref[1, :HALF, :] - packed(change)
    for s in range(out_ref.shape[0]):
        out_ref[s] = fresh


def level2_kernel(got_ref, core_ref, coeff0_ref, coeff1_ref, field_ref, left_ref, out_ref):
    change = mul(coeff0_ref[...], left_ref[0]) + mul(coeff1_ref[...], left_ref[1])
    coeff = coefficients([got_ref[:, 0], got_ref[:, 1]], core_ref)
    change = change + mul(coeff, left_ref[2])
    out_ref[...] = field_ref[...] - change


def whole(x):
    return pl.BlockSpec(x.shape, lambda i: (0,) * x.ndim)


def core_of(cores, level):
    return pl.BlockSpec((1, 1) + cores.shape[2:], lambda i: (0, level, 0, 0))


def call(kernel, out_shape, args, in_specs=None):
    if in_specs is None:
        in_specs = [whole(x) for x in args]
    single = not isinstance(out_shape[0], tuple)
    shapes = (out_shape,) if single else out_shape
    out = tuple(jax.ShapeDtypeStruct(s, jnp.float32) for s in shapes)
    specs = tuple(whole(o) for o in out)
    return pl.pallas_call(
        kernel,
        grid=(1,),
        out_shape=out[0] if single else out,
        in_specs=in_specs,
        out_specs=specs[0] if single else specs,
        compiler_params=pltpu.CompilerParams(vmem_limit_bytes=32 << 20),
    )(*args)


def swap(x, axes):
    return lax.all_to_all(x, axes, 0, 0, tiled=True)


def shards(rhs_field, right_basis, left_basis, cores):
    nz, nx = lax.axis_size("z"), lax.axis_size("x")
    ns = 2 * nx
    tile = (2 * HALF, LANES)
    half = (HALF, LANES)
    rhs, rank = rhs_field.shape[0], right_basis.shape[1]

    theirs, mine = gram_rows(rhs_field, right_basis, left_basis)
    theirs = lax.ppermute(theirs, "c", [(0, 1), (1, 0)])
    part = call(add_kernel, mine.shape, (mine, theirs))
    part = swap(part.reshape((nx * nz,) + tile), ("x", "z"))
    part = call(sum_spread_kernel, (nz,) + tile, (part,))
    blocks = swap(part, "z")

    send = jnp.broadcast_to(blocks[0, :HALF], (2 * ns,) + half)
    got = swap(send, ("y0",) + CHIP).reshape((2, ns) + half)
    coeff0, send = call(
        level0_kernel,
        ((rhs, rank), (4 * ns,) + half),
        (got, cores, blocks),
        [whole(got), core_of(cores, 0), whole(blocks)],
    )
    got = swap(send, ("y1", "y0") + CHIP).reshape((4, ns) + half)
    coeff1, send = call(
        level1_kernel,
        ((rhs, rank), (8,) + half),
        (got, cores, blocks, coeff0),
        [whole(got), core_of(cores, 1), whole(blocks), whole(coeff0)],
    )
    got = swap(send, LEAF)
    send = call(quads_kernel, (ns, 2) + half, (got,))
    got = swap(send, CHIP)
    return call(
        level2_kernel,
        rhs_field.shape,
        (got, cores, coeff0, coeff1, rhs_field, left_basis),
        [whole(got), core_of(cores, 2), whole(coeff0), whole(coeff1), whole(rhs_field), whole(left_basis)],
    )


def solution(mesh):
    nx, cores_of_chip = 4, 2
    nz = mesh.shape["row"] // (nx * cores_of_chip)
    points = LEAF + ("z", "x", "c")
    fine = Mesh(mesh.devices.reshape((2, 2, 2, nz, nx, cores_of_chip)), points)
    in_specs = (
        P(None, points),
        P(None, None, points),
        P(None, None, points),
        P(LEAF, None, None, None),
    )
    return jax.shard_map(shards, mesh=fine, in_specs=in_specs, out_specs=P(None, points), check_vma=False)
```

```python
import jax
import jax.numpy as jnp
from jax import lax
from jax.experimental import pallas as pl
from jax.experimental.pallas import tpu as pltpu
from jax.sharding import Mesh, PartitionSpec as P

LEAF = ("y2", "y1", "y0")
CHIP = ("c", "x")
HALF = 16
LANES = 128
BLOCKS = 8


def halves(a):
    high = a.astype(jnp.bfloat16)
    return high, (a - high.astype(jnp.float32)).astype(jnp.bfloat16)


def product(a, b, dims):
    def one(u, v):
        return lax.dot_general(u, v, (dims, ((), ())), preferred_element_type=jnp.float32)

    return one(a[0], b[0]) + (one(a[0], b[1]) + one(a[1], b[0]))


def mul(a, b):
    return product(halves(a), halves(b), ((1,), (0,)))


def mul_t(a, b):
    return product(halves(a), halves(b), ((1,), (1,)))


def stacked_product(a_high, a_low, b):
    rows = a_high.shape[0]

    def one(u, v):
        return lax.dot_general(u, v, (((1,), (1,)), ((), ())), preferred_element_type=jnp.float32)

    both = one(jnp.concatenate([a_high, a_low], axis=0), b[0])
    return both[:rows] + (both[rows:] + one(a_high, b[1]))


def gram_kernel(field_hbm, right_hbm, left_hbm, theirs_ref, mine_ref, field, right, left, sems):
    core = lax.axis_index("c")
    sides = (1 - core, core)
    outs = (theirs_ref, mine_ref)
    depth, _, _, rows, points = right.shape
    peers = mine_ref.shape[1]
    copies = []

    def fetch(src, dst):
        copy = pltpu.make_async_copy(src, dst, sems.at[len(copies)])
        copy.start()
        copies.append(copy)
        return copy

    def fetch_right(k):
        return [
            fetch(right_hbm.at[k, pl.ds(2 * rows * h + rows * side, rows), :], right.at[k, slot, h])
            for slot, side in enumerate(sides)
            for h in range(2)
        ]

    def fetch_left(j):
        part = left.shape[1] // 2
        return [fetch(left_hbm.at[j, pl.ds(part * i, part), :], left.at[j, pl.ds(part * i, part), :]) for i in range(2)]

    got_left, got_right = {}, {}
    got_left[0] = fetch_left(0)
    got_right[1] = fetch_right(1)
    got_right[2] = fetch_right(2)
    got_left[1] = fetch_left(1)
    got_field = fetch(field_hbm, field)
    got_right[0] = fetch_right(0)

    def arrived(waits):
        for copy in waits:
            copy.wait()

    def basis(k):
        arrived(got_right[k])
        return halves(right[k].reshape(4 * rows, points))

    def put(k, block, value):
        for slot, out_ref in enumerate(outs):
            for s in range(peers):
                for h in range(2):
                    first = 4 * rows * k + 2 * rows * slot + rows * h + HALF * s
                    piece = value[first : first + HALF]
                    out_ref[block, s, HALF * h : HALF * (h + 1), :] = piece[:, :LANES]
                    out_ref[block + 1, s, HALF * h : HALF * (h + 1), :] = piece[:, LANES:]

    def put_packed(k, value):
        for slot, out_ref in enumerate(outs):
            for s in range(peers):
                first = 4 * rows * k + 2 * rows * slot + HALF * s
                piece = [value[first + rows * h : first + rows * h + HALF] for h in range(2)]
                out_ref[k // 2, s, HALF * (k % 2) : HALF * (k % 2 + 1), :] = jnp.concatenate(piece, axis=1)

    for out_ref in outs:
        for s in range(peers):
            out_ref[1, s, HALF:, :] = jnp.zeros((HALF, LANES), jnp.float32)
    arrived(got_left[0])
    first_left = halves(left[0])
    one, two = basis(1), basis(2)
    high, low = (jnp.concatenate([one[i], two[i]], axis=0) for i in range(2))
    gram = stacked_product(high, low, first_left)
    put(0, 2, gram)
    put(1, 4, gram)
    arrived(got_left[1])
    put(0, 6, stacked_product(two[0], two[1], halves(left[1])))
    got_field.wait()
    zero = basis(0)
    high, low = (jnp.concatenate([zero[i], one[i], two[i]], axis=0) for i in range(2))
    proj = stacked_product(high, low, halves(field[...]))
    for k in range(depth):
        put_packed(k, proj)


def gram_rows(field, right, left):
    depth, rank, points = right.shape
    rows = rank // 4
    out = jax.ShapeDtypeStruct((BLOCKS, rows // HALF, 2 * HALF, LANES), jnp.float32)
    return pl.pallas_call(
        gram_kernel,
        out_shape=(out, out),
        in_specs=[pl.BlockSpec(memory_space=pltpu.HBM)] * 3,
        out_specs=(pl.BlockSpec(memory_space=pltpu.VMEM),) * 2,
        scratch_shapes=[
            pltpu.VMEM(field.shape, jnp.float32),
            pltpu.VMEM((depth, 2, 2, rows, points), jnp.float32),
            pltpu.VMEM((depth - 1, rank, points), jnp.float32),
            pltpu.SemaphoreType.DMA((1 + 4 * depth + 2 * (depth - 1),)),
        ],
        compiler_params=pltpu.CompilerParams(vmem_limit_bytes=54000 << 10),
    )(field, right, left)


def add_kernel(a_ref, b_ref, out_ref):
    out_ref[...] = a_ref[...] + b_ref[...]


def sum_spread_kernel(in_ref, out_ref):
    total = in_ref[0]
    for s in range(1, in_ref.shape[0]):
        total = total + in_ref[s]
    for s in range(out_ref.shape[0]):
        out_ref[s] = total


def coefficients(parts, core_ref):
    sides = []
    for part in parts:
        turned = part.reshape(LANES, LANES).T
        sides += [turned[: LANES // 2], turned[LANES // 2 :]]
    return mul(jnp.concatenate(sides, axis=1), core_ref[0, 0])


def two_sides(got_ref):
    group = got_ref.shape[0] // 2
    parts = []
    for side in range(2):
        part = got_ref[side * group]
        for g in range(1, group):
            part = part + got_ref[side * group + g]
        parts.append(part)
    return parts


def quads_kernel(got_ref, out_ref):
    group = got_ref.shape[1] // 2
    for side in range(2):
        part = got_ref[:, side * group]
        for g in range(1, group):
            part = part + got_ref[:, side * group + g]
        out_ref[side] = part


def packed(value):
    return jnp.concatenate([value[:HALF], value[HALF:]], axis=1)


def gram_block(blocks_ref, first):
    return jnp.concatenate([blocks_ref[first], blocks_ref[first + 1]], axis=1)


def level0_kernel(got_ref, core_ref, blocks_ref, coeff_ref, out_ref):
    coeff = coefficients(two_sides(got_ref), core_ref)
    coeff_ref[...] = coeff
    fresh = blocks_ref[0, HALF:, :] - packed(mul_t(gram_block(blocks_ref, 2), coeff))
    for s in range(out_ref.shape[0]):
        out_ref[s] = fresh


def level1_kernel(got_ref, core_ref, blocks_ref, coeff0_ref, coeff_ref, out_ref):
    coeff = coefficients(two_sides(got_ref), core_ref)
    coeff_ref[...] = coeff
    change = mul_t(gram_block(blocks_ref, 4), coeff0_ref[...])
    change = change + mul_t(gram_block(blocks_ref, 6), coeff)
    fresh = blocks_ref[1, :HALF, :] - packed(change)
    for s in range(out_ref.shape[0]):
        out_ref[s] = fresh


def base_kernel(coeff0_ref, coeff1_ref, field_ref, left_ref, out_ref):
    change = mul(coeff0_ref[...], left_ref[0]) + mul(coeff1_ref[...], left_ref[1])
    out_ref[...] = field_ref[...] - change


def level2_kernel(mine_ref, theirs_ref, core_ref, base_ref, left_ref, out_ref):
    first = lax.axis_index("c") == 0
    parts = []
    for side in range(2):
        mine, theirs = mine_ref[side], theirs_ref[side]
        parts.append(jnp.stack([jnp.where(first, mine, theirs), jnp.where(first, theirs, mine)]))
    coeff = coefficients(parts, core_ref)
    out_ref[...] = base_ref[...] - mul(coeff, left_ref[0])


def whole(x):
    return pl.BlockSpec(x.shape, lambda i: (0,) * x.ndim)


def core_of(cores, level):
    return pl.BlockSpec((1, 1) + cores.shape[2:], lambda i: (0, level, 0, 0))


def levels_of(basis, first, count):
    return pl.BlockSpec((count,) + basis.shape[1:], lambda i: (first // count, 0, 0))


def call(kernel, out_shape, args, in_specs=None):
    if in_specs is None:
        in_specs = [whole(x) for x in args]
    single = not isinstance(out_shape[0], tuple)
    shapes = (out_shape,) if single else out_shape
    out = tuple(jax.ShapeDtypeStruct(s, jnp.float32) for s in shapes)
    specs = tuple(whole(o) for o in out)
    return pl.pallas_call(
        kernel,
        grid=(1,),
        out_shape=out[0] if single else out,
        in_specs=in_specs,
        out_specs=specs[0] if single else specs,
        compiler_params=pltpu.CompilerParams(vmem_limit_bytes=32 << 20),
    )(*args)


def swap(x, axes):
    return lax.all_to_all(x, axes, 0, 0, tiled=True)


def shards(rhs_field, right_basis, left_basis, cores):
    nz, nx = lax.axis_size("z"), lax.axis_size("x")
    ns = 2 * nx
    tile = (2 * HALF, LANES)
    half = (HALF, LANES)
    rhs, rank = rhs_field.shape[0], right_basis.shape[1]

    theirs, mine = gram_rows(rhs_field, right_basis, left_basis)
    theirs = lax.ppermute(theirs, "c", [(0, 1), (1, 0)])
    part = call(add_kernel, mine.shape, (mine, theirs))
    part = swap(part.reshape((nz * nx,) + tile), ("z", "x"))
    part = call(sum_spread_kernel, (nz,) + tile, (part,))
    blocks = swap(part, "z")

    send = jnp.broadcast_to(blocks[0, :HALF], (2 * ns,) + half)
    got = swap(send, ("y0",) + CHIP).reshape((2, ns) + half)
    coeff0, send = call(
        level0_kernel,
        ((rhs, rank), (4 * ns,) + half),
        (got, cores, blocks),
        [whole(got), core_of(cores, 0), whole(blocks)],
    )
    got = swap(send, ("y1", "y0") + CHIP).reshape((4, ns) + half)
    coeff1, send = call(
        level1_kernel,
        ((rhs, rank), (8 * nx,) + half),
        (got, cores, blocks, coeff0),
        [whole(got), core_of(cores, 1), whole(blocks), whole(coeff0)],
    )
    got = swap(send, ("x",) + LEAF).reshape((nx, 8) + half)
    mine = call(quads_kernel, (2, nx) + half, (got,))
    theirs = lax.ppermute(mine, "c", [(0, 1), (1, 0)])
    base = call(
        base_kernel,
        rhs_field.shape,
        (coeff0, coeff1, rhs_field, left_basis),
        [whole(coeff0), whole(coeff1), whole(rhs_field), levels_of(left_basis, 0, 2)],
    )
    return call(
        level2_kernel,
        rhs_field.shape,
        (mine, theirs, cores, base, left_basis),
        [whole(mine), whole(theirs), core_of(cores, 2), whole(base), levels_of(left_basis, 2, 1)],
    )


def solution(mesh):
    nx, cores_of_chip = 4, 2
    nz = mesh.shape["row"] // (nx * cores_of_chip)
    points = LEAF + ("z", "x", "c")
    fine = Mesh(mesh.devices.reshape((2, 2, 2, nz, nx, cores_of_chip)), points)
    in_specs = (
        P(None, points),
        P(None, None, points),
        P(None, None, points),
        P(LEAF, None, None, None),
    )
    return jax.shard_map(shards, mesh=fine, in_specs=in_specs, out_specs=P(None, points), check_vma=False)
```

```python
import jax
import jax.numpy as jnp
from jax import lax
from jax.experimental import pallas as pl
from jax.experimental.pallas import tpu as pltpu
from jax.sharding import Mesh, PartitionSpec as P

LEAF = ("y2", "y1", "y0")
CHIP = ("c", "x")
HALF = 16
LANES = 128
BLOCKS = 8


def halves(a):
    high = a.astype(jnp.bfloat16)
    return high, (a - high.astype(jnp.float32)).astype(jnp.bfloat16)


def product(a, b, dims):
    def one(u, v):
        return lax.dot_general(u, v, (dims, ((), ())), preferred_element_type=jnp.float32)

    rows = a[0].shape[0]
    both = one(jnp.concatenate(a, axis=0), b[0])
    return both[:rows] + (both[rows:] + one(a[0], b[1]))


def product_t(a, b):
    return product(a, b, ((1,), (1,)))


def mul(a, b):
    return product(halves(a), halves(b), ((1,), (0,)))


def mul_t(a, b):
    return product_t(halves(a), halves(b))


def gram_kernel(field_hbm, right_hbm, left_hbm, theirs_ref, mine_ref, field, right, left, sems):
    first_core = lax.axis_index("c") == 0
    depth, rank, _ = right.shape
    rows = rank // 4
    peers = mine_ref.shape[1]
    copies = []

    def fetch(src, dst):
        copy = pltpu.make_async_copy(src, dst, sems.at[len(copies)])
        copy.start()
        copies.append(copy)

    fetch(left_hbm.at[0], left.at[0])
    fetch(right_hbm.at[1], right.at[1])
    fetch(right_hbm.at[2], right.at[2])
    fetch(left_hbm.at[1], left.at[1])
    fetch(field_hbm, field)
    fetch(right_hbm.at[0], right.at[0])

    def arrived(group):
        for copy in group:
            copy.wait()

    def basis(k):
        return halves(right[k])

    def pieces(value, s, h):
        first = 2 * rows * h + HALF * s
        zero, one = value[first : first + HALF], value[first + rows : first + rows + HALF]
        return jnp.where(first_core, zero, one), jnp.where(first_core, one, zero)

    def put(block, value):
        for s in range(peers):
            for h in range(2):
                for out_ref, piece in zip((mine_ref, theirs_ref), pieces(value, s, h)):
                    out_ref[block, s, HALF * h : HALF * (h + 1), :] = piece[:, :LANES]
                    out_ref[block + 1, s, HALF * h : HALF * (h + 1), :] = piece[:, LANES:]

    def put_packed(k, value):
        for s in range(peers):
            both = zip(pieces(value, s, 0), pieces(value, s, 1))
            for out_ref, piece in zip((mine_ref, theirs_ref), both):
                out_ref[k // 2, s, HALF * (k % 2) : HALF * (k % 2 + 1), :] = jnp.concatenate(piece, axis=1)

    for out_ref in (mine_ref, theirs_ref):
        for s in range(peers):
            out_ref[1, s, HALF:, :] = jnp.zeros((HALF, LANES), jnp.float32)
    arrived(copies[:3])
    left_0 = halves(left[0])
    right_1 = basis(1)
    put(2, product_t(right_1, left_0))
    right_2 = basis(2)
    put(4, product_t(right_2, left_0))
    arrived(copies[3:])
    put(6, product_t(right_2, halves(left[1])))
    rhs = halves(field[...])
    put_packed(1, product_t(right_1, rhs))
    put_packed(2, product_t(right_2, rhs))
    put_packed(0, product_t(basis(0), rhs))


def gram_rows(field, right, left):
    depth, rank, points = right.shape
    rows = rank // 4
    out = jax.ShapeDtypeStruct((BLOCKS, rows // HALF, 2 * HALF, LANES), jnp.float32)
    return pl.pallas_call(
        gram_kernel,
        out_shape=(out, out),
        in_specs=[pl.BlockSpec(memory_space=pltpu.HBM)] * 3,
        out_specs=(pl.BlockSpec(memory_space=pltpu.VMEM),) * 2,
        scratch_shapes=[
            pltpu.VMEM(field.shape, jnp.float32),
            pltpu.VMEM((depth, rank, points), jnp.float32),
            pltpu.VMEM((depth - 1, rank, points), jnp.float32),
            pltpu.SemaphoreType.DMA((2 * depth,)),
        ],
        compiler_params=pltpu.CompilerParams(vmem_limit_bytes=54000 << 10),
    )(field, right, left)


def add_kernel(a_ref, b_ref, out_ref):
    out_ref[...] = a_ref[...] + b_ref[...]


def sum_spread_kernel(in_ref, out_ref):
    total = in_ref[0]
    for s in range(1, in_ref.shape[0]):
        total = total + in_ref[s]
    for s in range(out_ref.shape[0]):
        out_ref[s] = total


def coefficients(parts, core_ref):
    sides = []
    for part in parts:
        turned = part.reshape(LANES, LANES).T
        sides += [turned[: LANES // 2], turned[LANES // 2 :]]
    return mul(jnp.concatenate(sides, axis=1), core_ref[0, 0])


def two_sides(got_ref):
    group = got_ref.shape[0] // 2
    parts = []
    for side in range(2):
        part = got_ref[side * group]
        for g in range(1, group):
            part = part + got_ref[side * group + g]
        parts.append(part)
    return parts


def quads_kernel(got_ref, out_ref):
    for side, part in enumerate(two_sides(got_ref)):
        for s in range(out_ref.shape[0]):
            out_ref[s, side] = part


def packed(value):
    return jnp.concatenate([value[:HALF], value[HALF:]], axis=1)


def gram_block(blocks_ref, first):
    return jnp.concatenate([blocks_ref[first], blocks_ref[first + 1]], axis=1)


def level0_kernel(got_ref, core_ref, blocks_ref, coeff_ref, out_ref):
    coeff = coefficients(two_sides(got_ref), core_ref)
    coeff_ref[...] = coeff
    fresh = blocks_ref[0, HALF:, :] - packed(mul_t(gram_block(blocks_ref, 2), coeff))
    for s in range(out_ref.shape[0]):
        out_ref[s] = fresh


def level1_kernel(got_ref, core_ref, blocks_ref, coeff0_ref, coeff_ref, out_ref):
    coeff = coefficients(two_sides(got_ref), core_ref)
    coeff_ref[...] = coeff
    change = mul_t(gram_block(blocks_ref, 4), coeff0_ref[...])
    change = change + mul_t(gram_block(blocks_ref, 6), coeff)
    fresh = blocks_ref[1, :HALF, :] - packed(change)
    for s in range(out_ref.shape[0]):
        out_ref[s] = fresh


def level2_kernel(got_ref, core_ref, coeff0_ref, coeff1_ref, field_ref, left_ref, out_ref):
    change = mul(coeff0_ref[...], left_ref[0]) + mul(coeff1_ref[...], left_ref[1])
    coeff = coefficients([got_ref[:, 0], got_ref[:, 1]], core_ref)
    change = change + mul(coeff, left_ref[2])
    out_ref[...] = field_ref[...] - change


def whole(x):
    return pl.BlockSpec(x.shape, lambda i: (0,) * x.ndim)


def core_of(cores, level):
    return pl.BlockSpec((1, 1) + cores.shape[2:], lambda i: (0, level, 0, 0))


def call(kernel, out_shape, args, in_specs=None):
    if in_specs is None:
        in_specs = [whole(x) for x in args]
    single = not isinstance(out_shape[0], tuple)
    shapes = (out_shape,) if single else out_shape
    out = tuple(jax.ShapeDtypeStruct(s, jnp.float32) for s in shapes)
    specs = tuple(whole(o) for o in out)
    return pl.pallas_call(
        kernel,
        grid=(1,),
        out_shape=out[0] if single else out,
        in_specs=in_specs,
        out_specs=specs[0] if single else specs,
        compiler_params=pltpu.CompilerParams(vmem_limit_bytes=32 << 20),
    )(*args)


def swap(x, axes):
    return lax.all_to_all(x, axes, 0, 0, tiled=True)


def shards(rhs_field, right_basis, left_basis, cores):
    nz, nx = lax.axis_size("z"), lax.axis_size("x")
    ns = 2 * nx
    tile = (2 * HALF, LANES)
    half = (HALF, LANES)
    rhs, rank = rhs_field.shape[0], right_basis.shape[1]

    theirs, mine = gram_rows(rhs_field, right_basis, left_basis)
    theirs = lax.ppermute(theirs, "c", [(0, 1), (1, 0)])
    part = call(add_kernel, mine.shape, (mine, theirs))
    part = swap(part.reshape((nz * nx,) + tile), ("z", "x"))
    part = call(sum_spread_kernel, (nz,) + tile, (part,))
    blocks = swap(part, "z")

    send = jnp.broadcast_to(blocks[0, :HALF], (2 * ns,) + half)
    got = swap(send, ("y0",) + CHIP).reshape((2, ns) + half)
    coeff0, send = call(
        level0_kernel,
        ((rhs, rank), (4 * ns,) + half),
        (got, cores, blocks),
        [whole(got), core_of(cores, 0), whole(blocks)],
    )
    got = swap(send, ("y1", "y0") + CHIP).reshape((4, ns) + half)
    coeff1, send = call(
        level1_kernel,
        ((rhs, rank), (8,) + half),
        (got, cores, blocks, coeff0),
        [whole(got), core_of(cores, 1), whole(blocks), whole(coeff0)],
    )
    got = swap(send, LEAF)
    send = call(quads_kernel, (ns, 2) + half, (got,))
    got = swap(send, CHIP)
    return call(
        level2_kernel,
        rhs_field.shape,
        (got, cores, coeff0, coeff1, rhs_field, left_basis),
        [whole(got), core_of(cores, 2), whole(coeff0), whole(coeff1), whole(rhs_field), whole(left_basis)],
    )


def solution(mesh):
    nx, cores_of_chip = 4, 2
    nz = mesh.shape["row"] // (nx * cores_of_chip)
    points = LEAF + ("z", "x", "c")
    fine = Mesh(mesh.devices.reshape((2, 2, 2, nz, nx, cores_of_chip)), points)
    in_specs = (
        P(None, points),
        P(None, None, points),
        P(None, None, points),
        P(LEAF, None, None, None),
    )
    return jax.shard_map(shards, mesh=fine, in_specs=in_specs, out_specs=P(None, points), check_vma=False)
```

```python
import jax
import jax.numpy as jnp
from jax import lax
from jax.experimental import pallas as pl
from jax.experimental.pallas import tpu as pltpu
from jax.sharding import Mesh, PartitionSpec as P

LEAF = ("y2", "y1", "y0")
CHIP = ("c", "x")
HALF = 16
LANES = 128
BLOCKS = 8


def halves(a):
    high = a.astype(jnp.bfloat16)
    return high, (a - high.astype(jnp.float32)).astype(jnp.bfloat16)


def product(a, b, dims):
    def one(u, v):
        return lax.dot_general(u, v, (dims, ((), ())), preferred_element_type=jnp.float32)

    rows = a[0].shape[0]
    both = one(jnp.concatenate(a, axis=0), b[0])
    return both[:rows] + (both[rows:] + one(a[0], b[1]))


def product_t(a, b):
    return product(a, b, ((1,), (1,)))


def mul(a, b):
    return product(halves(a), halves(b), ((1,), (0,)))


def mul_t(a, b):
    return product_t(halves(a), halves(b))


def gram_blocks(out_ref, right, left, field, first_group, second_group):
    depth, _, rows, points = right.shape
    peers = out_ref.shape[1]

    def basis(k):
        return halves(right[k].reshape(2 * rows, points))

    def put(block, value):
        for s in range(peers):
            for h in range(2):
                piece = value[rows * h + HALF * s : rows * h + HALF * (s + 1)]
                out_ref[block, s, HALF * h : HALF * (h + 1), :] = piece[:, :LANES]
                out_ref[block + 1, s, HALF * h : HALF * (h + 1), :] = piece[:, LANES:]

    def put_packed(k, value):
        for s in range(peers):
            pair = [value[rows * h + HALF * s : rows * h + HALF * (s + 1)] for h in range(2)]
            out_ref[k // 2, s, HALF * (k % 2) : HALF * (k % 2 + 1), :] = jnp.concatenate(pair, axis=1)

    for s in range(peers):
        out_ref[1, s, HALF:, :] = jnp.zeros((HALF, LANES), jnp.float32)
    for copy in first_group:
        copy.wait()
    left_0, right_1, right_2 = halves(left[0]), basis(1), basis(2)
    put(2, product_t(right_1, left_0))
    put(4, product_t(right_2, left_0))
    for copy in second_group:
        copy.wait()
    put(6, product_t(right_2, halves(left[1])))
    rhs = halves(field[...])
    put_packed(1, product_t(right_1, rhs))
    put_packed(2, product_t(right_2, rhs))
    put_packed(0, product_t(basis(0), rhs))


def theirs_kernel(field_hbm, right_hbm, left_hbm, theirs_ref, mine, left, field, right, sems):
    core = lax.axis_index("c")
    depth, _, rows, _ = right.shape
    copies = []

    def fetch(src, dst):
        copy = pltpu.make_async_copy(src, dst, sems.at[len(copies)])
        copy.start()
        copies.append(copy)

    def fetch_rows(k, side, dst):
        for h in range(2):
            fetch(right_hbm.at[k, pl.ds(rows * (2 * h + side), rows), :], dst.at[k, h])

    fetch(left_hbm.at[0], left.at[0])
    fetch_rows(1, 1 - core, right)
    fetch_rows(2, 1 - core, right)
    early = len(copies)
    fetch(left_hbm.at[1], left.at[1])
    fetch(field_hbm, field)
    fetch_rows(0, 1 - core, right)
    late = len(copies)
    for k in range(depth):
        fetch_rows(k, core, mine)
    gram_blocks(theirs_ref, right, left, field, copies[:early], copies[early:late])
    for copy in copies[late:]:
        copy.wait()


def mine_kernel(mine, left, field, out_ref):
    gram_blocks(out_ref, mine, left, field, (), ())


def gram_theirs(field, right, left):
    depth, rank, points = right.shape
    rows = rank // 4
    shapes = ((BLOCKS, rows // HALF, 2 * HALF, LANES), (depth, 2, rows, points), (depth - 1, rank, points), field.shape)
    return pl.pallas_call(
        theirs_kernel,
        out_shape=tuple(jax.ShapeDtypeStruct(s, jnp.float32) for s in shapes),
        in_specs=[pl.BlockSpec(memory_space=pltpu.HBM)] * 3,
        out_specs=(pl.BlockSpec(memory_space=pltpu.VMEM),) * 4,
        scratch_shapes=[
            pltpu.VMEM((depth, 2, rows, points), jnp.float32),
            pltpu.SemaphoreType.DMA((4 * depth + depth,)),
        ],
        compiler_params=pltpu.CompilerParams(vmem_limit_bytes=52000 << 10),
    )(field, right, left)


def add_kernel(a_ref, b_ref, out_ref):
    out_ref[...] = a_ref[...] + b_ref[...]


def sum_spread_kernel(in_ref, out_ref):
    total = in_ref[0]
    for s in range(1, in_ref.shape[0]):
        total = total + in_ref[s]
    for s in range(out_ref.shape[0]):
        out_ref[s] = total


def coefficients(parts, core_ref):
    sides = []
    for part in parts:
        turned = part.reshape(LANES, LANES).T
        sides += [turned[: LANES // 2], turned[LANES // 2 :]]
    return mul(jnp.concatenate(sides, axis=1), core_ref[0, 0])


def two_sides(got_ref):
    group = got_ref.shape[0] // 2
    parts = []
    for side in range(2):
        part = got_ref[side * group]
        for g in range(1, group):
            part = part + got_ref[side * group + g]
        parts.append(part)
    return parts


def quads_kernel(got_ref, out_ref):
    for side, part in enumerate(two_sides(got_ref)):
        for s in range(out_ref.shape[0]):
            out_ref[s, side] = part


def packed(value):
    return jnp.concatenate([value[:HALF], value[HALF:]], axis=1)


def gram_block(blocks_ref, first):
    return jnp.concatenate([blocks_ref[first], blocks_ref[first + 1]], axis=1)


def level0_kernel(got_ref, core_ref, blocks_ref, coeff_ref, out_ref):
    coeff = coefficients(two_sides(got_ref), core_ref)
    coeff_ref[...] = coeff
    fresh = blocks_ref[0, HALF:, :] - packed(mul_t(gram_block(blocks_ref, 2), coeff))
    for s in range(out_ref.shape[0]):
        out_ref[s] = fresh


def level1_kernel(got_ref, core_ref, blocks_ref, coeff0_ref, coeff_ref, out_ref):
    coeff = coefficients(two_sides(got_ref), core_ref)
    coeff_ref[...] = coeff
    change = mul_t(gram_block(blocks_ref, 4), coeff0_ref[...])
    change = change + mul_t(gram_block(blocks_ref, 6), coeff)
    fresh = blocks_ref[1, :HALF, :] - packed(change)
    for s in range(out_ref.shape[0]):
        out_ref[s] = fresh


def level2_kernel(got_ref, core_ref, coeff0_ref, coeff1_ref, field_ref, left_ref, out_ref):
    change = mul(coeff0_ref[...], left_ref[0]) + mul(coeff1_ref[...], left_ref[1])
    coeff = coefficients([got_ref[:, 0], got_ref[:, 1]], core_ref)
    change = change + mul(coeff, left_ref[2])
    out_ref[...] = field_ref[...] - change


def whole(x):
    return pl.BlockSpec(x.shape, lambda i: (0,) * x.ndim)


def core_of(cores, level):
    return pl.BlockSpec((1, 1) + cores.shape[2:], lambda i: (0, level, 0, 0))


def call(kernel, out_shape, args, in_specs=None):
    if in_specs is None:
        in_specs = [whole(x) for x in args]
    single = not isinstance(out_shape[0], tuple)
    shapes = (out_shape,) if single else out_shape
    out = tuple(jax.ShapeDtypeStruct(s, jnp.float32) for s in shapes)
    specs = tuple(whole(o) for o in out)
    return pl.pallas_call(
        kernel,
        grid=(1,),
        out_shape=out[0] if single else out,
        in_specs=in_specs,
        out_specs=specs[0] if single else specs,
        compiler_params=pltpu.CompilerParams(vmem_limit_bytes=32 << 20),
    )(*args)


def swap(x, axes):
    return lax.all_to_all(x, axes, 0, 0, tiled=True)


def shards(rhs_field, right_basis, left_basis, cores):
    nz, nx = lax.axis_size("z"), lax.axis_size("x")
    ns = 2 * nx
    tile = (2 * HALF, LANES)
    half = (HALF, LANES)
    rhs, rank = rhs_field.shape[0], right_basis.shape[1]

    theirs, *held = gram_theirs(rhs_field, right_basis, left_basis)
    theirs = lax.ppermute(theirs, "c", [(0, 1), (1, 0)])
    mine = call(mine_kernel, theirs.shape, tuple(held))
    part = call(add_kernel, mine.shape, (mine, theirs))
    part = swap(part.reshape((nz * nx,) + tile), ("z", "x"))
    part = call(sum_spread_kernel, (nz,) + tile, (part,))
    blocks = swap(part, "z")

    send = jnp.broadcast_to(blocks[0, :HALF], (2 * ns,) + half)
    got = swap(send, ("y0",) + CHIP).reshape((2, ns) + half)
    coeff0, send = call(
        level0_kernel,
        ((rhs, rank), (4 * ns,) + half),
        (got, cores, blocks),
        [whole(got), core_of(cores, 0), whole(blocks)],
    )
    got = swap(send, ("y1", "y0") + CHIP).reshape((4, ns) + half)
    coeff1, send = call(
        level1_kernel,
        ((rhs, rank), (8,) + half),
        (got, cores, blocks, coeff0),
        [whole(got), core_of(cores, 1), whole(blocks), whole(coeff0)],
    )
    got = swap(send, LEAF)
    send = call(quads_kernel, (ns, 2) + half, (got,))
    got = swap(send, CHIP)
    return call(
        level2_kernel,
        rhs_field.shape,
        (got, cores, coeff0, coeff1, rhs_field, left_basis),
        [whole(got), core_of(cores, 2), whole(coeff0), whole(coeff1), whole(rhs_field), whole(left_basis)],
    )


def solution(mesh):
    nx, cores_of_chip = 4, 2
    nz = mesh.shape["row"] // (nx * cores_of_chip)
    points = LEAF + ("z", "x", "c")
    fine = Mesh(mesh.devices.reshape((2, 2, 2, nz, nx, cores_of_chip)), points)
    in_specs = (
        P(None, points),
        P(None, None, points),
        P(None, None, points),
        P(LEAF, None, None, None),
    )
    return jax.shard_map(shards, mesh=fine, in_specs=in_specs, out_specs=P(None, points), check_vma=False)
```

```python
import jax
import jax.numpy as jnp
from jax import lax
from jax.experimental import pallas as pl
from jax.experimental.pallas import tpu as pltpu
from jax.sharding import Mesh, PartitionSpec as P

LEAF = ("y2", "y1", "y0")
CHIP = ("c", "x")
HALF = 16
LANES = 128
BLOCKS = 8


def halves(a):
    high = a.astype(jnp.bfloat16)
    return high, (a - high.astype(jnp.float32)).astype(jnp.bfloat16)


def product(a, b, dims):
    def one(u, v):
        return lax.dot_general(u, v, (dims, ((), ())), preferred_element_type=jnp.float32)

    rows = a[0].shape[0]
    both = one(jnp.concatenate(a, axis=0), b[0])
    return both[:rows] + (both[rows:] + one(a[0], b[1]))


def product_t(a, b):
    return product(a, b, ((1,), (1,)))


def mul(a, b):
    return product(halves(a), halves(b), ((1,), (0,)))


def mul_t(a, b):
    return product_t(halves(a), halves(b))


def gram_kernel(right, left, field, out_ref):
    depth, _, rows, points = right.shape
    peers = out_ref.shape[1]

    def basis(k):
        return halves(right[k].reshape(2 * rows, points))

    def put(block, value):
        for s in range(peers):
            for h in range(2):
                piece = value[rows * h + HALF * s : rows * h + HALF * (s + 1)]
                out_ref[block, s, HALF * h : HALF * (h + 1), :] = piece[:, :LANES]
                out_ref[block + 1, s, HALF * h : HALF * (h + 1), :] = piece[:, LANES:]

    def put_packed(k, value):
        for s in range(peers):
            pair = [value[rows * h + HALF * s : rows * h + HALF * (s + 1)] for h in range(2)]
            out_ref[k // 2, s, HALF * (k % 2) : HALF * (k % 2 + 1), :] = jnp.concatenate(pair, axis=1)

    for s in range(peers):
        out_ref[1, s, HALF:, :] = jnp.zeros((HALF, LANES), jnp.float32)
    left_0, right_1, right_2 = halves(left[0]), basis(1), basis(2)
    put(2, product_t(right_1, left_0))
    put(4, product_t(right_2, left_0))
    put(6, product_t(right_2, halves(left[1])))
    rhs = halves(field[...])
    put_packed(1, product_t(right_1, rhs))
    put_packed(2, product_t(right_2, rhs))
    put_packed(0, product_t(basis(0), rhs))


def fetch_kernel(right_hbm, left_hbm, theirs, mine, left, sems):
    core = lax.axis_index("c")
    depth, _, rows, _ = mine.shape
    copies = []

    def fetch(src, dst):
        copy = pltpu.make_async_copy(src, dst, sems.at[len(copies)])
        copy.start()
        copies.append(copy)

    for j in range(left.shape[0]):
        fetch(left_hbm.at[j], left.at[j])
    for k in range(depth):
        for side, dst in ((1 - core, theirs), (core, mine)):
            for h in range(2):
                fetch(right_hbm.at[k, pl.ds(rows * (2 * h + side), rows), :], dst.at[k, h])
    for copy in copies:
        copy.wait()


def fetch_bases(right, left):
    depth, rank, points = right.shape
    rows = jax.ShapeDtypeStruct((depth, 2, rank // 4, points), jnp.float32)
    return pl.pallas_call(
        fetch_kernel,
        out_shape=(rows, rows, jax.ShapeDtypeStruct((depth - 1, rank, points), jnp.float32)),
        in_specs=[pl.BlockSpec(memory_space=pltpu.HBM)] * 2,
        out_specs=(pl.BlockSpec(memory_space=pltpu.VMEM),) * 3,
        scratch_shapes=[pltpu.SemaphoreType.DMA((4 * depth + depth - 1,))],
        compiler_params=pltpu.CompilerParams(vmem_limit_bytes=52000 << 10),
    )(right, left)


def add_kernel(a_ref, b_ref, out_ref):
    out_ref[...] = a_ref[...] + b_ref[...]


def sum_spread_kernel(in_ref, out_ref):
    total = in_ref[0]
    for s in range(1, in_ref.shape[0]):
        total = total + in_ref[s]
    for s in range(out_ref.shape[0]):
        out_ref[s] = total


def coefficients(parts, core_ref):
    sides = []
    for part in parts:
        turned = part.reshape(LANES, LANES).T
        sides += [turned[: LANES // 2], turned[LANES // 2 :]]
    return mul(jnp.concatenate(sides, axis=1), core_ref[0, 0])


def two_sides(got_ref):
    group = got_ref.shape[0] // 2
    parts = []
    for side in range(2):
        part = got_ref[side * group]
        for g in range(1, group):
            part = part + got_ref[side * group + g]
        parts.append(part)
    return parts


def quads_kernel(got_ref, out_ref):
    for side, part in enumerate(two_sides(got_ref)):
        for s in range(out_ref.shape[0]):
            out_ref[s, side] = part


def packed(value):
    return jnp.concatenate([value[:HALF], value[HALF:]], axis=1)


def gram_block(blocks_ref, first):
    return jnp.concatenate([blocks_ref[first], blocks_ref[first + 1]], axis=1)


def level0_kernel(got_ref, core_ref, blocks_ref, coeff_ref, out_ref):
    coeff = coefficients(two_sides(got_ref), core_ref)
    coeff_ref[...] = coeff
    fresh = blocks_ref[0, HALF:, :] - packed(mul_t(gram_block(blocks_ref, 2), coeff))
    for s in range(out_ref.shape[0]):
        out_ref[s] = fresh


def level1_kernel(got_ref, core_ref, blocks_ref, coeff0_ref, coeff_ref, out_ref):
    coeff = coefficients(two_sides(got_ref), core_ref)
    coeff_ref[...] = coeff
    change = mul_t(gram_block(blocks_ref, 4), coeff0_ref[...])
    change = change + mul_t(gram_block(blocks_ref, 6), coeff)
    fresh = blocks_ref[1, :HALF, :] - packed(change)
    for s in range(out_ref.shape[0]):
        out_ref[s] = fresh


def level2_kernel(got_ref, core_ref, coeff0_ref, coeff1_ref, field_ref, left_ref, out_ref):
    change = mul(coeff0_ref[...], left_ref[0]) + mul(coeff1_ref[...], left_ref[1])
    coeff = coefficients([got_ref[:, 0], got_ref[:, 1]], core_ref)
    change = change + mul(coeff, left_ref[2])
    out_ref[...] = field_ref[...] - change


def whole(x):
    return pl.BlockSpec(x.shape, lambda i: (0,) * x.ndim)


def core_of(cores, level):
    return pl.BlockSpec((1, 1) + cores.shape[2:], lambda i: (0, level, 0, 0))


def call(kernel, out_shape, args, in_specs=None):
    if in_specs is None:
        in_specs = [whole(x) for x in args]
    single = not isinstance(out_shape[0], tuple)
    shapes = (out_shape,) if single else out_shape
    out = tuple(jax.ShapeDtypeStruct(s, jnp.float32) for s in shapes)
    specs = tuple(whole(o) for o in out)
    return pl.pallas_call(
        kernel,
        grid=(1,),
        out_shape=out[0] if single else out,
        in_specs=in_specs,
        out_specs=specs[0] if single else specs,
        compiler_params=pltpu.CompilerParams(vmem_limit_bytes=32 << 20),
    )(*args)


def swap(x, axes):
    return lax.all_to_all(x, axes, 0, 0, tiled=True)


def shards(rhs_field, right_basis, left_basis, cores):
    nz, nx = lax.axis_size("z"), lax.axis_size("x")
    ns = 2 * nx
    tile = (2 * HALF, LANES)
    half = (HALF, LANES)
    rhs, rank = rhs_field.shape[0], right_basis.shape[1]

    their_rows, my_rows, left = fetch_bases(right_basis, left_basis)
    gram = (BLOCKS, nx, 2 * HALF, LANES)
    theirs = call(gram_kernel, gram, (their_rows, left, rhs_field))
    theirs = lax.ppermute(theirs, "c", [(0, 1), (1, 0)])
    mine = call(gram_kernel, gram, (my_rows, left, rhs_field))
    part = call(add_kernel, mine.shape, (mine, theirs))
    part = swap(part.reshape((nz * nx,) + tile), ("z", "x"))
    part = call(sum_spread_kernel, (nz,) + tile, (part,))
    blocks = swap(part, "z")

    send = jnp.broadcast_to(blocks[0, :HALF], (2 * ns,) + half)
    got = swap(send, ("y0",) + CHIP).reshape((2, ns) + half)
    coeff0, send = call(
        level0_kernel,
        ((rhs, rank), (4 * ns,) + half),
        (got, cores, blocks),
        [whole(got), core_of(cores, 0), whole(blocks)],
    )
    got = swap(send, ("y1", "y0") + CHIP).reshape((4, ns) + half)
    coeff1, send = call(
        level1_kernel,
        ((rhs, rank), (8,) + half),
        (got, cores, blocks, coeff0),
        [whole(got), core_of(cores, 1), whole(blocks), whole(coeff0)],
    )
    got = swap(send, LEAF)
    send = call(quads_kernel, (ns, 2) + half, (got,))
    got = swap(send, CHIP)
    return call(
        level2_kernel,
        rhs_field.shape,
        (got, cores, coeff0, coeff1, rhs_field, left_basis),
        [whole(got), core_of(cores, 2), whole(coeff0), whole(coeff1), whole(rhs_field), whole(left_basis)],
    )


def solution(mesh):
    nx, cores_of_chip = 4, 2
    nz = mesh.shape["row"] // (nx * cores_of_chip)
    points = LEAF + ("z", "x", "c")
    fine = Mesh(mesh.devices.reshape((2, 2, 2, nz, nx, cores_of_chip)), points)
    in_specs = (
        P(None, points),
        P(None, None, points),
        P(None, None, points),
        P(LEAF, None, None, None),
    )
    return jax.shard_map(shards, mesh=fine, in_specs=in_specs, out_specs=P(None, points), check_vma=False)
```

```python
import jax
import jax.numpy as jnp
from jax import lax
from jax.experimental import pallas as pl
from jax.experimental.pallas import tpu as pltpu
from jax.sharding import Mesh, PartitionSpec as P

LEAF = ("y2", "y1", "y0")
CHIP = ("c", "x")
HALF = 16
LANES = 128
BLOCKS = 8


def halves(a):
    high = a.astype(jnp.bfloat16)
    return high, (a - high.astype(jnp.float32)).astype(jnp.bfloat16)


def product(a, b, dims):
    def one(u, v):
        return lax.dot_general(u, v, (dims, ((), ())), preferred_element_type=jnp.float32)

    rows = a[0].shape[0]
    both = one(jnp.concatenate(a, axis=0), b[0])
    return both[:rows] + (both[rows:] + one(a[0], b[1]))


def product_t(a, b):
    return product(a, b, ((1,), (1,)))


def mul(a, b):
    return product(halves(a), halves(b), ((1,), (0,)))


def mul_t(a, b):
    return product_t(halves(a), halves(b))


def gram_kernel(right, left, field, out_ref):
    depth, _, rows, points = right.shape
    peers = out_ref.shape[1]

    def basis(k):
        return halves(right[k].reshape(2 * rows, points))

    def put(block, value):
        for s in range(peers):
            for h in range(2):
                piece = value[rows * h + HALF * s : rows * h + HALF * (s + 1)]
                out_ref[block, s, HALF * h : HALF * (h + 1), :] = piece[:, :LANES]
                out_ref[block + 1, s, HALF * h : HALF * (h + 1), :] = piece[:, LANES:]

    def put_packed(k, value):
        for s in range(peers):
            pair = [value[rows * h + HALF * s : rows * h + HALF * (s + 1)] for h in range(2)]
            out_ref[k // 2, s, HALF * (k % 2) : HALF * (k % 2 + 1), :] = jnp.concatenate(pair, axis=1)

    for s in range(peers):
        out_ref[1, s, HALF:, :] = jnp.zeros((HALF, LANES), jnp.float32)
    left_0, right_1, right_2 = halves(left[0]), basis(1), basis(2)
    put(2, product_t(right_1, left_0))
    put(4, product_t(right_2, left_0))
    put(6, product_t(right_2, halves(left[1])))
    rhs = halves(field[...])
    put_packed(1, product_t(right_1, rhs))
    put_packed(2, product_t(right_2, rhs))
    put_packed(0, product_t(basis(0), rhs))


def fetch_kernel(right_hbm, left_hbm, theirs, mine, left, sems):
    core = lax.axis_index("c")
    depth = mine.shape[0]
    copies = []

    def fetch(src, dst):
        copy = pltpu.make_async_copy(src, dst, sems.at[len(copies)])
        copy.start()
        copies.append(copy)

    for j in range(left.shape[0]):
        fetch(left_hbm.at[j], left.at[j])
    for k in range(depth):
        for side, dst in ((1 - core, theirs), (core, mine)):
            fetch(right_hbm.at[k, :, side], dst.at[k])
    for copy in copies:
        copy.wait()


def fetch_bases(right, left):
    depth, rank, points = right.shape
    rows = jax.ShapeDtypeStruct((depth, 2, rank // 4, points), jnp.float32)
    return pl.pallas_call(
        fetch_kernel,
        out_shape=(rows, rows, jax.ShapeDtypeStruct((depth - 1, rank, points), jnp.float32)),
        in_specs=[pl.BlockSpec(memory_space=pltpu.HBM)] * 2,
        out_specs=(pl.BlockSpec(memory_space=pltpu.VMEM),) * 3,
        scratch_shapes=[pltpu.SemaphoreType.DMA((2 * depth + depth - 1,))],
        compiler_params=pltpu.CompilerParams(vmem_limit_bytes=52000 << 10),
    )(right.reshape(depth, 2, 2, rank // 4, points), left)


def add_kernel(a_ref, b_ref, out_ref):
    out_ref[...] = a_ref[...] + b_ref[...]


def sum_spread_kernel(in_ref, out_ref):
    total = in_ref[0]
    for s in range(1, in_ref.shape[0]):
        total = total + in_ref[s]
    for s in range(out_ref.shape[0]):
        out_ref[s] = total


def coefficients(parts, core_ref):
    sides = []
    for part in parts:
        turned = part.reshape(LANES, LANES).T
        sides += [turned[: LANES // 2], turned[LANES // 2 :]]
    return mul(jnp.concatenate(sides, axis=1), core_ref[0, 0])


def two_sides(got_ref):
    group = got_ref.shape[0] // 2
    parts = []
    for side in range(2):
        part = got_ref[side * group]
        for g in range(1, group):
            part = part + got_ref[side * group + g]
        parts.append(part)
    return parts


def quads_kernel(got_ref, out_ref):
    for side, part in enumerate(two_sides(got_ref)):
        for s in range(out_ref.shape[0]):
            out_ref[s, side] = part


def packed(value):
    return jnp.concatenate([value[:HALF], value[HALF:]], axis=1)


def gram_block(blocks_ref, first):
    return jnp.concatenate([blocks_ref[first], blocks_ref[first + 1]], axis=1)


def level0_kernel(got_ref, core_ref, blocks_ref, coeff_ref, out_ref):
    coeff = coefficients(two_sides(got_ref), core_ref)
    coeff_ref[...] = coeff
    fresh = blocks_ref[0, HALF:, :] - packed(mul_t(gram_block(blocks_ref, 2), coeff))
    for s in range(out_ref.shape[0]):
        out_ref[s] = fresh


def level1_kernel(got_ref, core_ref, blocks_ref, coeff0_ref, coeff_ref, out_ref):
    coeff = coefficients(two_sides(got_ref), core_ref)
    coeff_ref[...] = coeff
    change = mul_t(gram_block(blocks_ref, 4), coeff0_ref[...])
    change = change + mul_t(gram_block(blocks_ref, 6), coeff)
    fresh = blocks_ref[1, :HALF, :] - packed(change)
    for s in range(out_ref.shape[0]):
        out_ref[s] = fresh


def level2_kernel(got_ref, core_ref, coeff0_ref, coeff1_ref, field_ref, left_ref, out_ref):
    change = mul(coeff0_ref[...], left_ref[0]) + mul(coeff1_ref[...], left_ref[1])
    coeff = coefficients([got_ref[:, 0], got_ref[:, 1]], core_ref)
    change = change + mul(coeff, left_ref[2])
    out_ref[...] = field_ref[...] - change


def whole(x):
    return pl.BlockSpec(x.shape, lambda i: (0,) * x.ndim)


def core_of(cores, level):
    return pl.BlockSpec((1, 1) + cores.shape[2:], lambda i: (0, level, 0, 0))


def call(kernel, out_shape, args, in_specs=None):
    if in_specs is None:
        in_specs = [whole(x) for x in args]
    single = not isinstance(out_shape[0], tuple)
    shapes = (out_shape,) if single else out_shape
    out = tuple(jax.ShapeDtypeStruct(s, jnp.float32) for s in shapes)
    specs = tuple(whole(o) for o in out)
    return pl.pallas_call(
        kernel,
        grid=(1,),
        out_shape=out[0] if single else out,
        in_specs=in_specs,
        out_specs=specs[0] if single else specs,
        compiler_params=pltpu.CompilerParams(vmem_limit_bytes=32 << 20),
    )(*args)


def swap(x, axes):
    return lax.all_to_all(x, axes, 0, 0, tiled=True)


def shards(rhs_field, right_basis, left_basis, cores):
    nz, nx = lax.axis_size("z"), lax.axis_size("x")
    ns = 2 * nx
    tile = (2 * HALF, LANES)
    half = (HALF, LANES)
    rhs, rank = rhs_field.shape[0], right_basis.shape[1]

    their_rows, my_rows, left = fetch_bases(right_basis, left_basis)
    gram = (BLOCKS, nx, 2 * HALF, LANES)
    theirs = call(gram_kernel, gram, (their_rows, left, rhs_field))
    theirs = lax.ppermute(theirs, "c", [(0, 1), (1, 0)])
    mine = call(gram_kernel, gram, (my_rows, left, rhs_field))
    part = call(add_kernel, mine.shape, (mine, theirs))
    part = swap(part.reshape((nz * nx,) + tile), ("z", "x"))
    part = call(sum_spread_kernel, (nz,) + tile, (part,))
    blocks = swap(part, "z")

    send = jnp.broadcast_to(blocks[0, :HALF], (2 * ns,) + half)
    got = swap(send, ("y0",) + CHIP).reshape((2, ns) + half)
    coeff0, send = call(
        level0_kernel,
        ((rhs, rank), (4 * ns,) + half),
        (got, cores, blocks),
        [whole(got), core_of(cores, 0), whole(blocks)],
    )
    got = swap(send, ("y1", "y0") + CHIP).reshape((4, ns) + half)
    coeff1, send = call(
        level1_kernel,
        ((rhs, rank), (8,) + half),
        (got, cores, blocks, coeff0),
        [whole(got), core_of(cores, 1), whole(blocks), whole(coeff0)],
    )
    got = swap(send, LEAF)
    send = call(quads_kernel, (ns, 2) + half, (got,))
    got = swap(send, CHIP)
    return call(
        level2_kernel,
        rhs_field.shape,
        (got, cores, coeff0, coeff1, rhs_field, left_basis),
        [whole(got), core_of(cores, 2), whole(coeff0), whole(coeff1), whole(rhs_field), whole(left_basis)],
    )


def solution(mesh):
    nx, cores_of_chip = 4, 2
    nz = mesh.shape["row"] // (nx * cores_of_chip)
    points = LEAF + ("z", "x", "c")
    fine = Mesh(mesh.devices.reshape((2, 2, 2, nz, nx, cores_of_chip)), points)
    in_specs = (
        P(None, points),
        P(None, None, points),
        P(None, None, points),
        P(LEAF, None, None, None),
    )
    return jax.shard_map(shards, mesh=fine, in_specs=in_specs, out_specs=P(None, points), check_vma=False)
```

```python
import jax
import jax.numpy as jnp
from jax import lax
from jax.experimental import pallas as pl
from jax.experimental.pallas import tpu as pltpu
from jax.sharding import Mesh, PartitionSpec as P

LEAF = ("y2", "y1", "y0")
CHIP = ("c", "x")
HALF = 16
LANES = 128
BLOCKS = 8


def halves(a):
    high = a.astype(jnp.bfloat16)
    return high, (a - high.astype(jnp.float32)).astype(jnp.bfloat16)


def product(a, b, dims):
    def one(u, v):
        return lax.dot_general(u, v, (dims, ((), ())), preferred_element_type=jnp.float32)

    rows = a[0].shape[0]
    both = one(jnp.concatenate(a, axis=0), b[0])
    return both[:rows] + (both[rows:] + one(a[0], b[1]))


def product_t(a, b):
    return product(a, b, ((1,), (1,)))


def mul(a, b):
    return product(halves(a), halves(b), ((1,), (0,)))


def mul_t(a, b):
    return product_t(halves(a), halves(b))


def gram_kernel(right, left, field, out_ref):
    depth, _, rows, points = right.shape
    peers = out_ref.shape[1]

    def basis(k):
        return halves(right[k].reshape(2 * rows, points))

    def put(block, value):
        for s in range(peers):
            for h in range(2):
                piece = value[rows * h + HALF * s : rows * h + HALF * (s + 1)]
                out_ref[block, s, HALF * h : HALF * (h + 1), :] = piece[:, :LANES]
                out_ref[block + 1, s, HALF * h : HALF * (h + 1), :] = piece[:, LANES:]

    def put_packed(k, value):
        for s in range(peers):
            pair = [value[rows * h + HALF * s : rows * h + HALF * (s + 1)] for h in range(2)]
            out_ref[k // 2, s, HALF * (k % 2) : HALF * (k % 2 + 1), :] = jnp.concatenate(pair, axis=1)

    for s in range(peers):
        out_ref[1, s, HALF:, :] = jnp.zeros((HALF, LANES), jnp.float32)
    left_0, right_1, right_2 = halves(left[0]), basis(1), basis(2)
    put(2, product_t(right_1, left_0))
    put(4, product_t(right_2, left_0))
    put(6, product_t(right_2, halves(left[1])))
    rhs = halves(field[...])
    put_packed(1, product_t(right_1, rhs))
    put_packed(2, product_t(right_2, rhs))
    put_packed(0, product_t(basis(0), rhs))


def fetch_kernel(right_hbm, left_hbm, theirs, mine, left, sems):
    core = lax.axis_index("c")
    depth = mine.shape[0]
    copies = []

    def fetch(src, dst):
        copy = pltpu.make_async_copy(src, dst, sems.at[len(copies)])
        copy.start()
        copies.append(copy)

    for j in range(left.shape[0]):
        fetch(left_hbm.at[j], left.at[j])
    for k in range(depth):
        for side, dst in ((1 - core, theirs), (core, mine)):
            fetch(right_hbm.at[k, :, side], dst.at[k])
    for copy in copies:
        copy.wait()


def fetch_bases(right, left):
    depth, rank, points = right.shape
    rows = jax.ShapeDtypeStruct((depth, 2, rank // 4, points), jnp.float32)
    return pl.pallas_call(
        fetch_kernel,
        out_shape=(rows, rows, jax.ShapeDtypeStruct((depth - 1, rank, points), jnp.float32)),
        in_specs=[pl.BlockSpec(memory_space=pltpu.HBM)] * 2,
        out_specs=(pl.BlockSpec(memory_space=pltpu.VMEM),) * 3,
        scratch_shapes=[pltpu.SemaphoreType.DMA((2 * depth + depth - 1,))],
        compiler_params=pltpu.CompilerParams(vmem_limit_bytes=52000 << 10),
    )(right.reshape(depth, 2, 2, rank // 4, points), left)


def add_kernel(a_ref, b_ref, out_ref):
    out_ref[...] = a_ref[...] + b_ref[...]


def sum_spread_kernel(in_ref, out_ref):
    total = in_ref[0]
    for s in range(1, in_ref.shape[0]):
        total = total + in_ref[s]
    for s in range(out_ref.shape[0]):
        out_ref[s] = total


def coefficients(parts, core_ref):
    sides = []
    for part in parts:
        turned = part.reshape(LANES, LANES).T
        sides += [turned[: LANES // 2], turned[LANES // 2 :]]
    return mul(jnp.concatenate(sides, axis=1), core_ref[0, 0])


def two_sides(got_ref):
    group = got_ref.shape[0] // 2
    parts = []
    for side in range(2):
        part = got_ref[side * group]
        for g in range(1, group):
            part = part + got_ref[side * group + g]
        parts.append(part)
    return parts


def quads_kernel(got_ref, out_ref):
    for side, part in enumerate(two_sides(got_ref)):
        for s in range(out_ref.shape[0]):
            out_ref[s, side] = part


def packed(value):
    return jnp.concatenate([value[:HALF], value[HALF:]], axis=1)


def gram_block(blocks_ref, first):
    return jnp.concatenate([blocks_ref[first], blocks_ref[first + 1]], axis=1)


def level0_kernel(got_ref, core_ref, blocks_ref, coeff_ref, out_ref):
    coeff = coefficients(two_sides(got_ref), core_ref)
    coeff_ref[...] = coeff
    fresh = blocks_ref[0, HALF:, :] - packed(mul_t(gram_block(blocks_ref, 2), coeff))
    for s in range(out_ref.shape[0]):
        out_ref[s] = fresh


def level1_kernel(got_ref, core_ref, blocks_ref, coeff0_ref, coeff_ref, out_ref):
    coeff = coefficients(two_sides(got_ref), core_ref)
    coeff_ref[...] = coeff
    change = mul_t(gram_block(blocks_ref, 4), coeff0_ref[...])
    change = change + mul_t(gram_block(blocks_ref, 6), coeff)
    fresh = blocks_ref[1, :HALF, :] - packed(change)
    for s in range(out_ref.shape[0]):
        out_ref[s] = fresh


def level2_kernel(got_ref, core_ref, coeff0_ref, coeff1_ref, field_ref, left_ref, out_ref):
    coeff = coefficients([got_ref[:, 0], got_ref[:, 1]], core_ref)
    levels = jnp.concatenate([coeff0_ref[...], coeff1_ref[...], coeff], axis=1)
    left = left_ref[...].reshape(levels.shape[1], field_ref.shape[1])
    out_ref[...] = field_ref[...] - mul(levels, left)


def whole(x):
    return pl.BlockSpec(x.shape, lambda i: (0,) * x.ndim)


def core_of(cores, level):
    return pl.BlockSpec((1, 1) + cores.shape[2:], lambda i: (0, level, 0, 0))


def call(kernel, out_shape, args, in_specs=None):
    if in_specs is None:
        in_specs = [whole(x) for x in args]
    single = not isinstance(out_shape[0], tuple)
    shapes = (out_shape,) if single else out_shape
    out = tuple(jax.ShapeDtypeStruct(s, jnp.float32) for s in shapes)
    specs = tuple(whole(o) for o in out)
    return pl.pallas_call(
        kernel,
        grid=(1,),
        out_shape=out[0] if single else out,
        in_specs=in_specs,
        out_specs=specs[0] if single else specs,
        compiler_params=pltpu.CompilerParams(vmem_limit_bytes=32 << 20),
    )(*args)


def swap(x, axes):
    return lax.all_to_all(x, axes, 0, 0, tiled=True)


def shards(rhs_field, right_basis, left_basis, cores):
    nz, nx = lax.axis_size("z"), lax.axis_size("x")
    ns = 2 * nx
    tile = (2 * HALF, LANES)
    half = (HALF, LANES)
    rhs, rank = rhs_field.shape[0], right_basis.shape[1]

    their_rows, my_rows, left = fetch_bases(right_basis, left_basis)
    gram = (BLOCKS, nx, 2 * HALF, LANES)
    theirs = call(gram_kernel, gram, (their_rows, left, rhs_field))
    theirs = lax.ppermute(theirs, "c", [(0, 1), (1, 0)])
    mine = call(gram_kernel, gram, (my_rows, left, rhs_field))
    part = call(add_kernel, mine.shape, (mine, theirs))
    part = swap(part.reshape((nz * nx,) + tile), ("z", "x"))
    part = call(sum_spread_kernel, (nz,) + tile, (part,))
    blocks = swap(part, "z")

    send = jnp.broadcast_to(blocks[0, :HALF], (2 * ns,) + half)
    got = swap(send, ("y0",) + CHIP).reshape((2, ns) + half)
    coeff0, send = call(
        level0_kernel,
        ((rhs, rank), (4 * ns,) + half),
        (got, cores, blocks),
        [whole(got), core_of(cores, 0), whole(blocks)],
    )
    got = swap(send, ("y1", "y0") + CHIP).reshape((4, ns) + half)
    coeff1, send = call(
        level1_kernel,
        ((rhs, rank), (8,) + half),
        (got, cores, blocks, coeff0),
        [whole(got), core_of(cores, 1), whole(blocks), whole(coeff0)],
    )
    got = swap(send, LEAF)
    send = call(quads_kernel, (ns, 2) + half, (got,))
    got = swap(send, CHIP)
    return call(
        level2_kernel,
        rhs_field.shape,
        (got, cores, coeff0, coeff1, rhs_field, left_basis),
        [whole(got), core_of(cores, 2), whole(coeff0), whole(coeff1), whole(rhs_field), whole(left_basis)],
    )


def solution(mesh):
    nx, cores_of_chip = 4, 2
    nz = mesh.shape["row"] // (nx * cores_of_chip)
    points = LEAF + ("z", "x", "c")
    fine = Mesh(mesh.devices.reshape((2, 2, 2, nz, nx, cores_of_chip)), points)
    in_specs = (
        P(None, points),
        P(None, None, points),
        P(None, None, points),
        P(LEAF, None, None, None),
    )
    return jax.shard_map(shards, mesh=fine, in_specs=in_specs, out_specs=P(None, points), check_vma=False)
```
